32 devices in a mesh: seq: 16 (over z, y, core), head: 2 (over x).
Axes of the slice: x: 2, y: 2, z: 4, core: 2. Of those that a mesh axis runs over, the one named last changes fastest.
Arguments:
- query: bfloat16 [4096, 2048], P('seq', 'head'), may hold values from -40 to 40
- key_in: bfloat16 [4096, 2048], P('seq', 'head'), may hold values from -6 to 6
- value: bfloat16 [4096, 2048], P('seq', 'head'), may hold values from -40 to 40
- cotangent: bfloat16 [4096, 2048], P('seq', 'head'), may hold values from -6 to 6
Outputs:
- output: bfloat16 [4096, 2048], P('seq', 'head')
- grad_query: bfloat16 [4096, 2048], P('seq', 'head')
- grad_key: bfloat16 [4096, 2048], P('seq', 'head')
- grad_value: bfloat16 [4096, 2048], P('seq', 'head')
The draws below stay inside these ranges and needn't reach their ends.
All inputs are finite; a program needn't handle non-finite values.
Results may differ from the reference program's by a relative error of at most 0.0059.
Values sent between devices are 32-bit elements; how exact they have to be, the bound alone decides.
No kernel may reach another device: no remote copies, remote signals or barrier semaphores. Data moves between devices by JAX's collectives and lax.ppermute only.
A program may use at most 128 MiB of HBM per device.

```python
import math
import jax
import jax.numpy as jnp
from jax import lax

HEADS = 16
HEAD_DIM = 128
TOK_DEV = 256
TOKENS = 4096
FEATURES = 2048


def draw_query(key, part):
    first, second = jax.random.split(jax.random.fold_in(key, 11))
    shape = (TOKENS, HEADS * HEAD_DIM)
    base = jnp.clip(jax.random.normal(first, shape, jnp.float32), -4.0, 4.0)
    scales = jnp.exp(jax.random.uniform(second, (TOKENS, 1), jnp.float32, 0.0, math.log(10.0)))
    return (base * scales).astype(jnp.bfloat16)


def draw_value(key, part):
    first, second = jax.random.split(jax.random.fold_in(key, 23))
    shape = (TOKENS, HEADS * HEAD_DIM)
    offsets = jax.random.uniform(second, (HEADS,), jnp.float32, 0.0, 1.0)
    heads = jnp.arange(HEADS, dtype=jnp.float32)
    head_scale = jnp.exp(math.log(10.0) * (heads + offsets) / HEADS)
    columns = jnp.repeat(head_scale, HEAD_DIM)[None, :]
    base = jnp.clip(jax.random.normal(first, shape, jnp.float32), -4.0, 4.0)
    return (base * columns).astype(jnp.bfloat16)


def shard_levels(stream_key, dims, shards, least, high):
    loudness = 1.0
    for axis_at, shards_of in shards:
        draws = jax.random.uniform(jax.random.fold_in(jax.random.fold_in(stream_key, 6), axis_at), (shards_of,), jnp.float32, least / len(shards), high / len(shards))
        loudness = loudness * jnp.repeat(jnp.exp(draws), dims[axis_at] // shards_of).reshape((-1,) + (1,) * (len(dims) - 1 - axis_at))
    return loudness


def centred(key, extent, spread, bound, cuts=(), held_as=jnp.bfloat16):
    result = spread * jax.random.normal(key, extent, jnp.float32)
    if cuts:
        result = result * shard_levels(key, extent, cuts, -0.22, 0.18)
    return jnp.clip(result, -bound, bound).astype(held_as)


def setup_inputs(seed: int = 0) -> dict:
    key_list = jax.random.split(jax.random.key(seed), 5)
    query = draw_query(jax.random.fold_in(key_list[4], 71), 0)
    key_in = centred(key_list[1], (TOKENS, FEATURES), 1.0, 6.0, ((0, 16), (1, 2)))
    value = draw_value(jax.random.fold_in(key_list[4], 71), 0)
    cotangent = centred(key_list[3], (TOKENS, FEATURES), 1.0, 6.0, ((0, 16), (1, 2)))
    return {"query": query, "key_in": key_in, "value": value, "cotangent": cotangent}


def reference(query, key_in, value, cotangent):
    blocks = query.shape[0] // TOK_DEV
    width = HEADS * HEAD_DIM

    def split(arr):
        return arr.reshape(blocks, TOK_DEV, HEADS, HEAD_DIM)
    qb, kb, vb, cb = (split(query), split(key_in), split(value), split(cotangent))
    rows = jnp.arange(TOK_DEV, dtype=jnp.int32)
    mask = rows[:, None] >= rows[None, :]

    def forward(prefix, items):
        q, k, v, c = items
        qf, kf, vf, cf = (q.astype(jnp.float32), k.astype(jnp.float32), v.astype(jnp.float32), c.astype(jnp.float32))
        prefix_b = prefix.astype(jnp.bfloat16)
        raw = jnp.einsum('thd,shd->hts', qf, kf)
        scores = jnp.where(mask[None], raw, 0.0).astype(jnp.bfloat16)
        mixed = jnp.einsum('hts,she->the', scores.astype(jnp.float32), vf) + jnp.einsum('thd,hde->the', qf, prefix_b.astype(jnp.float32))
        square = lax.optimization_barrier(jnp.sum(mixed * mixed, axis=(1, 2)))
        rstd = lax.rsqrt(square / width + 1e-06)
        output = (mixed * rstd[:, None, None]).astype(jnp.bfloat16)
        mean_dot = lax.optimization_barrier(jnp.sum(cf * mixed, axis=(1, 2))) / width
        d_mixed = (rstd[:, None, None] * (cf - mixed * (rstd * rstd * mean_dot)[:, None, None])).astype(jnp.bfloat16)
        state = jnp.einsum('thd,the->hde', kf, vf)
        return (prefix + state, (output, d_mixed, prefix_b))
    start = jnp.zeros((HEADS, HEAD_DIM, HEAD_DIM), jnp.float32)
    last, (output, d_all, prefix_all) = lax.scan(forward, start, (qb, kb, vb, cb))

    def backward(suffix, items):
        q, k, v, d, prefix_b = items
        qf, kf, vf, df = (q.astype(jnp.float32), k.astype(jnp.float32), v.astype(jnp.float32), d.astype(jnp.float32))
        pf = prefix_b.astype(jnp.float32)
        suffix_b = suffix.astype(jnp.bfloat16).astype(jnp.float32)
        raw = jnp.einsum('thd,shd->hts', qf, kf)
        scores = jnp.where(mask[None], raw, 0.0).astype(jnp.bfloat16).astype(jnp.float32)
        d_raw = jnp.einsum('the,she->hts', df, vf)
        d_scores = jnp.where(mask[None], d_raw, 0.0).astype(jnp.bfloat16).astype(jnp.float32)
        grad_q = jnp.einsum('hts,shd->thd', d_scores, kf) + jnp.einsum('the,hde->thd', df, pf)
        grad_k = jnp.einsum('hts,thd->shd', d_scores, qf) + jnp.einsum('she,hde->shd', vf, suffix_b)
        grad_v = jnp.einsum('hts,the->she', scores, df) + jnp.einsum('shd,hde->she', kf, suffix_b)
        grad_state = jnp.einsum('thd,the->hde', qf, df)
        outs = (grad_q.astype(jnp.bfloat16), grad_k.astype(jnp.bfloat16), grad_v.astype(jnp.bfloat16))
        return (suffix + grad_state, outs)
    first, (grad_q, grad_k, grad_v) = lax.scan(backward, start, (qb, kb, vb, d_all, prefix_all), reverse=True)
    total = query.shape[0]
    return (output.reshape(total, width), grad_q.reshape(total, width), grad_k.reshape(total, width), grad_v.reshape(total, width))
```

```python
import jax
import jax.numpy as jnp
from jax import lax
from jax.experimental import pallas as pl
from jax.experimental.pallas import tpu as pltpu
from jax.sharding import PartitionSpec as P

HEAD_DIM = 128
EPS = 1e-06
F32 = jnp.float32
BF16 = jnp.bfloat16


def first_head(quarter, per):
    block = lax.axis_index("seq")
    core = block % 2
    pair = (block // 2) % 2
    if quarter >= 2:
        core = 1 - core
    if quarter % 2:
        pair = 1 - pair
    return (2 * core + pair) * per


def head_columns(quarter, sub, per):
    return pl.ds(pl.multiple_of((first_head(quarter, per) + sub) * HEAD_DIM, HEAD_DIM), HEAD_DIM)


def spots(per, quarters=range(4)):
    return [(quarter, sub, (quarter % 2) * per + sub) for quarter in quarters for sub in range(per)]


def dot(a, b, contract):
    return lax.dot_general(a, b, (contract, ((), ())), preferred_element_type=F32)


def causal(rows):
    return lax.broadcasted_iota(jnp.int32, (rows, rows), 0) >= lax.broadcasted_iota(jnp.int32, (rows, rows), 1)


def call(kernel, outs, args, flops, scratch=()):
    moved = sum(a.size * a.dtype.itemsize for a in (*args, *outs))
    return pl.pallas_call(
        kernel,
        out_shape=outs,
        in_specs=[pl.BlockSpec(memory_space=pltpu.VMEM)] * len(args),
        out_specs=[pl.BlockSpec(memory_space=pltpu.VMEM)] * len(outs),
        scratch_shapes=list(scratch),
        cost_estimate=pl.CostEstimate(flops=int(flops), bytes_accessed=int(moved), transcendentals=0),
        compiler_params=pltpu.CompilerParams(vmem_limit_bytes=16 * 1024 * 1024),
    )(*args)


def like(shape, dtype=F32):
    return jax.ShapeDtypeStruct(tuple(shape), dtype)


def exchange(axis, pairs_of, array):
    count = lax.axis_size(axis)
    return lax.ppermute(array, axis, [(i, pairs_of(i)) for i in range(count)])


def far_scan(total, reverse):
    count = lax.axis_size("seq")
    steps = count // 4
    far = lax.axis_index("seq") // 4
    if reverse:
        far = steps - 1 - far
    before = jnp.zeros_like(total)
    hop = 1
    if steps & (steps - 1) == 0:
        while hop < steps:
            got = exchange("seq", lambda i: i ^ (4 * hop), total)
            before = before + jnp.where((far // hop) % 2 == 1, got, 0.0)
            total = total + got
            hop *= 2
        return before
    while hop < steps:
        up = [(i, i + 4 * hop) for i in range(count - 4 * hop)]
        got = lax.ppermute(total, "seq", [(d, s) for s, d in up] if reverse else up)
        before = before + got
        total = total + got
        hop *= 2
    return before


def scan(keep, send, reverse):
    block = lax.axis_index("seq")
    core, pair = block % 2, (block // 2) % 2
    if reverse:
        core, pair = 1 - core, 1 - pair
    got = exchange("seq", lambda i: i ^ 1, send)
    chip = keep + got
    other = exchange("seq", lambda i: i ^ 2, chip[1])
    before = far_scan(chip[0] + other, reverse)
    theirs = before + jnp.where(pair == 0, chip[0], 0.0)
    mine = before + jnp.where(pair == 1, other, 0.0)
    back = exchange("seq", lambda i: i ^ 2, theirs)
    base = jnp.stack([mine, back])
    away = exchange("seq", lambda i: i ^ 1, base + jnp.where(core == 0, keep, 0.0))
    return base + jnp.where(core == 1, got, 0.0), away


def local(query, key_in, value, cotangent):
    rows, width = query.shape
    heads = width // HEAD_DIM
    per = heads // 4
    features = width * lax.axis_size("head")
    half = (2, per * HEAD_DIM, HEAD_DIM)
    state_flops = heads * rows * HEAD_DIM * HEAD_DIM

    def states_of(quarters):
        def kernel(a_ref, b_ref, out_ref):
            for quarter, sub, _ in spots(per, quarters):
                cols = head_columns(quarter, sub, per)
                out_ref[quarter % 2, sub * HEAD_DIM : (sub + 1) * HEAD_DIM, :] = dot(a_ref[:, cols], b_ref[:, cols], ((0,), (0,)))

        return kernel

    (send,) = call(states_of((2, 3)), [like(half)], (key_in, value), state_flops)
    (keep,) = call(states_of((0, 1)), [like(half)], (key_in, value), state_flops)

    def inner(q_ref, k_ref, v_ref, scores_ref, near_ref):
        mask = causal(rows)
        for head in range(heads):
            cols = slice(head * HEAD_DIM, (head + 1) * HEAD_DIM)
            raw = dot(q_ref[:, cols], k_ref[:, cols], ((1,), (1,)))
            scores = jnp.where(mask, raw, 0.0).astype(BF16)
            scores_ref[head] = scores
            near_ref[:, cols] = dot(scores, v_ref[:, cols], ((1,), (0,)))

    scores, near = call(
        inner,
        [like((heads, rows, rows), BF16), like((rows, width))],
        (query, key_in, value),
        4 * heads * rows * rows * HEAD_DIM,
    )

    own, away = scan(keep, send, False)

    def mix(q_ref, c_ref, near_ref, own_ref, away_ref, mixed_ref, stats_ref):
        square = jnp.zeros((rows, HEAD_DIM), F32)
        along = jnp.zeros((rows, HEAD_DIM), F32)
        for quarter, sub, _ in spots(per):
            cols = head_columns(quarter, sub, per)
            prefix_ref = own_ref if quarter < 2 else away_ref
            prefix = prefix_ref[quarter % 2, sub * HEAD_DIM : (sub + 1) * HEAD_DIM, :].astype(BF16)
            mixed = near_ref[:, cols] + dot(q_ref[:, cols], prefix, ((1,), (0,)))
            mixed_ref[:, cols] = mixed
            square += mixed * mixed
            along += c_ref[:, cols].astype(F32) * mixed
        stats_ref[0:1, :] = jnp.sum(square.T, axis=0, keepdims=True)
        stats_ref[1:2, :] = jnp.sum(along.T, axis=0, keepdims=True)

    mixed, stats = call(
        mix, [like((rows, width)), like((2, rows))], (query, cotangent, near, own, away), 2 * state_flops
    )
    if lax.axis_size("head") == 2:
        stats = stats + exchange("head", lambda i: 1 - i, stats)
    else:
        stats = lax.psum(stats, "head")

    def token_scales(stats_ref):
        rstd = lax.rsqrt(stats_ref[0:1, :] / features + EPS)
        slope = rstd * rstd * (stats_ref[1:2, :] / features)
        return (
            jnp.broadcast_to(rstd, (HEAD_DIM, rows)).T,
            jnp.broadcast_to(slope, (HEAD_DIM, rows)).T,
        )

    def grads_of(quarters):
        def kernel(q_ref, c_ref, mixed_ref, stats_ref, d_ref, out_ref):
            rstd, slope = token_scales(stats_ref)
            for quarter, sub, spot in spots(per, quarters):
                cols = head_columns(quarter, sub, per)
                d_mixed = (rstd * (c_ref[:, cols].astype(F32) - mixed_ref[:, cols] * slope)).astype(BF16)
                d_ref[:, spot * HEAD_DIM : (spot + 1) * HEAD_DIM] = d_mixed
                out_ref[quarter % 2, sub * HEAD_DIM : (sub + 1) * HEAD_DIM, :] = dot(q_ref[:, cols], d_mixed, ((0,), (0,)))

        return kernel

    d_half = like((rows, width // 2), BF16)
    d_send, g_send = call(grads_of((2, 3)), [d_half, like(half)], (query, cotangent, mixed, stats), state_flops)
    d_keep, g_keep = call(grads_of((0, 1)), [d_half, like(half)], (query, cotangent, mixed, stats), state_flops)

    def middle(
        q_ref, k_ref, v_ref, scores_ref, mixed_ref, stats_ref, d_keep_ref, d_send_ref, own_ref, away_ref,
        out_ref, gq_ref, gk_ref, gv_ref,
    ):
        mask = causal(rows)
        rstd, _ = token_scales(stats_ref)
        for quarter, sub, spot in spots(per):
            cols = head_columns(quarter, sub, per)
            d_ref, prefix_ref = (d_keep_ref, own_ref) if quarter < 2 else (d_send_ref, away_ref)
            out_ref[:, cols] = (mixed_ref[:, cols] * rstd).astype(BF16)
            d_mixed = d_ref[:, spot * HEAD_DIM : (spot + 1) * HEAD_DIM]
            prefix = prefix_ref[quarter % 2, sub * HEAD_DIM : (sub + 1) * HEAD_DIM, :].astype(BF16)
            raw = dot(d_mixed, v_ref[:, cols], ((1,), (1,)))
            d_scores = jnp.where(mask, raw, 0.0).astype(BF16)
            gq = dot(d_scores, k_ref[:, cols], ((1,), (0,))) + dot(d_mixed, prefix, ((1,), (1,)))
            gq_ref[:, cols] = gq.astype(BF16)
            gk_ref[:, cols] = dot(d_scores, q_ref[:, cols], ((0,), (0,)))
            gv_ref[:, cols] = dot(scores_ref[first_head(quarter, per) + sub], d_mixed, ((0,), (0,)))

    whole = like((rows, width), BF16)
    output, grad_q, near_k, near_v = call(
        middle,
        [whole, whole, like((rows, width)), like((rows, width))],
        (query, key_in, value, scores, mixed, stats, d_keep, d_send, own, away),
        8 * heads * rows * rows * HEAD_DIM,
    )

    g_own, g_away = scan(g_keep, g_send, True)

    def last(k_ref, v_ref, near_k_ref, near_v_ref, own_ref, away_ref, gk_ref, gv_ref):
        for quarter, sub, _ in spots(per):
            cols = head_columns(quarter, sub, per)
            suffix_ref = own_ref if quarter < 2 else away_ref
            suffix = suffix_ref[quarter % 2, sub * HEAD_DIM : (sub + 1) * HEAD_DIM, :].astype(BF16)
            gk_ref[:, cols] = (near_k_ref[:, cols] + dot(v_ref[:, cols], suffix, ((1,), (1,)))).astype(BF16)
            gv_ref[:, cols] = (near_v_ref[:, cols] + dot(k_ref[:, cols], suffix, ((1,), (0,)))).astype(BF16)

    grad_k, grad_v = call(last, [whole, whole], (key_in, value, near_k, near_v, g_own, g_away), 4 * state_flops)
    return output, grad_q, grad_k, grad_v


def solution(mesh):
    spec = P("seq", "head")
    return jax.shard_map(local, mesh=mesh, in_specs=(spec,) * 4, out_specs=(spec,) * 4, check_vma=False)
```

```python
import jax
import jax.numpy as jnp
from jax import lax
from jax.experimental import pallas as pl
from jax.experimental.pallas import tpu as pltpu
from jax.sharding import PartitionSpec as P

HEAD_DIM = 128
EPS = 1e-06
CHUNKS = 2
F32 = jnp.float32
BF16 = jnp.bfloat16
VMEM = pl.BlockSpec(memory_space=pltpu.VMEM)
HBM = pl.BlockSpec(memory_space=pltpu.HBM)

OWN, AWAY = 0, 1


class Layout:
    def __init__(self, rows, heads):
        self.rows = rows
        self.per = heads // 4
        self.chunks = CHUNKS if self.per % CHUNKS == 0 else 1
        self.hc = self.per // self.chunks
        self.half = jax.ShapeDtypeStruct((2, self.hc * HEAD_DIM, HEAD_DIM), F32)

    def heads(self, half):
        block = lax.axis_index("seq")
        core, pair = block & 1, (block >> 1) & 1
        if half == AWAY:
            core = 1 - core
        out = []
        for sub in range(self.per):
            for second in range(2):
                head = (2 * core + (1 - pair if second else pair)) * self.per + sub
                chunk, slot = divmod(sub, self.hc)
                spot = second * self.per + sub
                out.append((head, chunk, (second, pl.ds(slot * HEAD_DIM, HEAD_DIM)), pl.ds(spot * HEAD_DIM, HEAD_DIM)))
        return out


    def quarters(self, half):
        block = lax.axis_index("seq")
        core, pair = block & 1, (block >> 1) & 1
        if half == AWAY:
            core = 1 - core
        size = self.per * HEAD_DIM
        return [
            (pl.ds(pl.multiple_of((2 * core + (1 - pair if second else pair)) * size, HEAD_DIM), size), pl.ds(second * size, size))
            for second in range(2)
        ]


def columns(head):
    return pl.ds(pl.multiple_of(head * HEAD_DIM, HEAD_DIM), HEAD_DIM)


def dot(a, b, contract):
    return lax.dot_general(a, b, (contract, ((), ())), preferred_element_type=F32)


def causal(rows):
    return lax.broadcasted_iota(jnp.int32, (rows, rows), 0) >= lax.broadcasted_iota(jnp.int32, (rows, rows), 1)


def like(shape, dtype=F32):
    return jax.ShapeDtypeStruct(tuple(shape), dtype)


def call(kernel, outs, args, flops, in_hbm=(), out_hbm=(), scratch=(), alias=None):
    moved = sum(a.size * a.dtype.itemsize for a in (*args, *outs))
    return pl.pallas_call(
        kernel,
        out_shape=outs,
        in_specs=[HBM if i in in_hbm else VMEM for i in range(len(args))],
        out_specs=[HBM if i in out_hbm else VMEM for i in range(len(outs))],
        scratch_shapes=list(scratch),
        input_output_aliases=alias or {},
        cost_estimate=pl.CostEstimate(flops=int(flops), bytes_accessed=int(moved), transcendentals=0),
        compiler_params=pltpu.CompilerParams(vmem_limit_bytes=16 * 1024 * 1024),
    )(*[pltpu.with_memory_space_constraint(a, pltpu.HBM) if i in in_hbm else a for i, a in enumerate(args)])


def exchange(axis, partner, array):
    return lax.ppermute(array, axis, [(i, partner(i)) for i in range(lax.axis_size(axis))])


def hops(count):
    steps = count // 4
    by_xor = steps & (steps - 1) == 0
    out, hop = [], 1
    while hop < steps:
        out.append(hop)
        hop *= 2
    return out, by_xor


def scan(keep, send, reverse, beside):
    count = lax.axis_size("seq")
    block = lax.axis_index("seq")
    core, pair, far = block & 1, (block >> 1) & 1, block >> 2
    if reverse:
        core, pair, far = 1 - core, 1 - pair, count // 4 - 1 - far
    each = range(len(keep))
    extra = {}

    def beside_of(name, ready, come):
        if name not in beside:
            return come
        come, extra[name] = lax.optimization_barrier((come, beside[name](ready, extra)))
        return come

    got = [exchange("seq", lambda i: i ^ 1, s) for s in send]
    chip = [keep[c] + got[c] for c in each]
    edge = [jnp.where(core == 0, keep[c], got[c]) for c in each]
    other = [exchange("seq", lambda i: i ^ 2, chip[c][1]) for c in each]
    other = beside_of("pair", chip, other)
    total = [chip[c][0] + other[c] for c in each]
    pair_edge = [jnp.where(pair == 0, chip[c][0], other[c]) for c in each]
    before = [jnp.zeros_like(t) for t in total]
    steps, by_xor = hops(count)
    for hop in steps:
        if by_xor:
            come = [exchange("seq", lambda i: i ^ (4 * hop), t) for t in total]
        else:
            up = [(i, i + 4 * hop) for i in range(count - 4 * hop)]
            if reverse:
                up = [(d, s) for s, d in up]
            come = [lax.ppermute(t, "seq", up) for t in total]
        if hop == steps[0]:
            come = beside_of("first", total, come)
        if hop == steps[-1]:
            come = beside_of("last", total, come)
        if by_xor:
            before = [b + jnp.where(far & hop != 0, g, 0.0) for b, g in zip(before, come)]
        else:
            before = [b + g for b, g in zip(before, come)]
        total = [t + g for t, g in zip(total, come)]
    theirs = [before[c] + jnp.where(pair == 0, pair_edge[c], 0.0) for c in each]
    mine = [before[c] + jnp.where(pair == 1, pair_edge[c], 0.0) for c in each]
    back = [exchange("seq", lambda i: i ^ 2, t) for t in theirs]
    base = [jnp.stack([mine[c], back[c]]) for c in each]
    away = [exchange("seq", lambda i: i ^ 1, base[c] + jnp.where(core == 0, edge[c], 0.0)) for c in each]
    own = [base[c] + jnp.where(core == 1, edge[c], 0.0) for c in each]
    return own, away, extra


def after(early, *arrays):
    return lax.optimization_barrier((early, arrays))[1]


def local(query, key_in, value, cotangent):
    rows, width = query.shape
    heads = width // HEAD_DIM
    lay = Layout(rows, heads)
    n = lay.chunks
    features = width * lax.axis_size("head")
    half_wide = width // 2
    state_flops = heads * rows * HEAD_DIM * HEAD_DIM
    block_flops = heads * rows * rows * HEAD_DIM
    whole = like((rows, width), BF16)
    wide = like((rows, half_wide))

    def loads(half, sources, targets, sems):
        return [
            [
                pltpu.make_async_copy(a.at[:, there], b.at[:, here], sems.at[second, j])
                for j, (a, b) in enumerate(zip(sources, targets))
            ]
            for second, (there, here) in enumerate(lay.quarters(half))
        ]

    def start(copies):
        for copy in copies:
            copy.start()

    def wait(copies):
        for copy in copies:
            copy.wait()

    packed = like((rows, half_wide), BF16)

    def first_states(k_any, v_any, k_own_ref, v_own_ref, k_ref, v_ref, *refs):
        outs, (own_sems, sems) = refs[:n], refs[n:]
        near = loads(OWN, (k_any, v_any), (k_own_ref, v_own_ref), own_sems)
        copies = loads(AWAY, (k_any, v_any), (k_ref, v_ref), sems)
        for part in copies + near:
            start(part)
        arrived = set()
        for head, chunk, place, spot in sorted(lay.heads(AWAY), key=lambda h: h[2][0]):
            if place[0] not in arrived:
                arrived.add(place[0])
                wait(copies[place[0]])
            outs[chunk][place] = dot(k_ref[:, spot], v_ref[:, spot], ((0,), (0,)))
        for part in near:
            wait(part)

    k_own, v_own, k_away, v_away, *send = call(
        first_states,
        [packed] * 4 + [lay.half] * n,
        (key_in, value),
        state_flops,
        (0, 1),
        (),
        [pltpu.SemaphoreType.DMA((2, 2))] * 2,
    )

    def second_states(k_ref, v_ref, *outs):
        for _, chunk, place, spot in lay.heads(OWN):
            outs[chunk][place] = dot(k_ref[:, spot], v_ref[:, spot], ((0,), (0,)))

    keep = call(second_states, [lay.half] * n, (k_own, v_own), state_flops)

    def inner(ready, _):
        def kernel(q_ref, *refs):
            mask = causal(rows)
            for half in (OWN, AWAY):
                k_ref, v_ref, near_ref = refs[half], refs[2 + half], refs[4 + half]
                for head, _, _, spot in lay.heads(half):
                    scores = jnp.where(mask, dot(q_ref[:, columns(head)], k_ref[:, spot], ((1,), (1,))), 0.0).astype(BF16)
                    near_ref[:, spot] = dot(scores, v_ref[:, spot], ((1,), (0,)))

        args = after(ready, query, k_own, k_away, v_own, v_away)
        return call(kernel, [wide] * 2, args, 4 * block_flops)

    own, away, extra = scan(keep, send, False, {"pair": inner})
    near = extra["pair"]

    def mix(half, prefix):
        def kernel(q_ref, c_ref, near_ref, *refs):
            prefix_refs, (mixed_ref, stats_ref, rounded_ref) = refs[:n], refs[n:]
            square = jnp.zeros((rows, HEAD_DIM), F32)
            along = jnp.zeros((rows, HEAD_DIM), F32)
            for head, chunk, place, spot in lay.heads(half):
                cols = columns(head)
                prefix_b = prefix_refs[chunk][place].astype(BF16)
                rounded_ref[spot, :] = prefix_b
                mixed = near_ref[:, spot] + dot(q_ref[:, cols], prefix_b, ((1,), (0,)))
                mixed_ref[:, spot] = mixed
                square += mixed * mixed
                along += c_ref[:, cols].astype(F32) * mixed
            stats_ref[0:1, :] = jnp.sum(square.T, axis=0, keepdims=True)
            stats_ref[1:2, :] = jnp.sum(along.T, axis=0, keepdims=True)

        args = (query, cotangent, near[half], *prefix)
        outs = [wide, like((2, rows)), like((half_wide, HEAD_DIM), BF16)]
        return call(kernel, outs, args, state_flops, alias={2: 0})

    mixed_own, stats_own, prefix_own = mix(OWN, own)
    mixed_away, stats_away, prefix_away = mix(AWAY, away)
    mixed = (mixed_own, mixed_away)
    stats = stats_own + stats_away
    if lax.axis_size("head") == 2:
        stats = stats + exchange("head", lambda i: 1 - i, stats)
    else:
        stats = lax.psum(stats, "head")

    def token_scales(stats_ref):
        rstd = lax.rsqrt(stats_ref[0:1, :] / features + EPS)
        slope = rstd * rstd * (stats_ref[1:2, :] / features)
        return (
            jnp.broadcast_to(rstd, (HEAD_DIM, rows)).T,
            jnp.broadcast_to(slope, (HEAD_DIM, rows)).T,
        )

    def grads(half):
        def kernel(q_ref, c_ref, mixed_ref, stats_ref, d_ref, *outs):
            rstd, slope = token_scales(stats_ref)
            for head, chunk, place, spot in lay.heads(half):
                cols = columns(head)
                d_mixed = (rstd * (c_ref[:, cols].astype(F32) - mixed_ref[:, spot] * slope)).astype(BF16)
                d_ref[:, spot] = d_mixed
                outs[chunk][place] = dot(q_ref[:, cols], d_mixed, ((0,), (0,)))

        out = call(
            kernel,
            [like((rows, half_wide), BF16)] + [lay.half] * n,
            (query, cotangent, mixed[half], stats),
            state_flops,
        )
        return out[0], out[1:]

    d_away, g_send = grads(AWAY)
    d_own, g_keep = grads(OWN)

    def emit(ready, _):
        def kernel(stats_ref, own_ref, away_ref, q_any, k_any, v_any, out_any, q_ref, k_ref, v_ref, *scratch):
            in_sems, out_ref, out_sems = scratch
            copies = loads(OWN, (q_any, k_any, v_any), (q_ref, k_ref, v_ref), in_sems)
            for part in copies:
                start(part)
            rstd, _ = token_scales(stats_ref)
            for half, mixed_ref in ((OWN, own_ref), (AWAY, away_ref)):
                for second, (there, here) in enumerate(lay.quarters(half)):
                    i = 2 * half + second
                    for sub in range(lay.per):
                        part = pl.ds(sub * HEAD_DIM, HEAD_DIM)
                        spot = pl.ds((second * lay.per + sub) * HEAD_DIM, HEAD_DIM)
                        out_ref[i, :, part] = (mixed_ref[:, spot] * rstd).astype(BF16)
                    copy = pltpu.make_async_copy(out_ref.at[i], out_any.at[:, there], out_sems.at[i])
                    copy.start()
                    copies.append([copy])
            for part in copies:
                wait(part)

        args = after(ready, stats, *mixed, query, key_in, value)
        scratch = [
            pltpu.SemaphoreType.DMA((2, 3)),
            pltpu.VMEM((4, rows, lay.per * HEAD_DIM), BF16),
            pltpu.SemaphoreType.DMA((4,)),
        ]
        return call(kernel, [whole, packed, packed, packed], args, width * rows, (3, 4, 5), (0,), scratch)

    def middle_head(q, k, v, d, prefix, mask, spot, gq_ref, gk_ref, gv_ref):
        scores = jnp.where(mask, dot(q, k, ((1,), (1,))), 0.0).astype(BF16)
        d_scores = jnp.where(mask, dot(d, v, ((1,), (1,))), 0.0).astype(BF16)
        gq_ref[:, spot] = (dot(d_scores, k, ((1,), (0,))) + dot(d, prefix, ((1,), (1,)))).astype(BF16)
        gk_ref[:, spot] = dot(d_scores, q, ((0,), (0,)))
        gv_ref[:, spot] = dot(scores, d, ((0,), (0,)))

    def middle_own(ready, extra):
        def kernel(q_ref, k_ref, v_ref, d_ref, prefix_ref, *outs):
            mask = causal(rows)
            for _, _, _, spot in lay.heads(OWN):
                middle_head(
                    q_ref[:, spot], k_ref[:, spot], v_ref[:, spot], d_ref[:, spot], prefix_ref[spot, :], mask, spot, *outs
                )

        args = after(ready, *extra["pair"][1:], d_own, prefix_own)
        return call(kernel, [packed, wide, wide], args, 5 * block_flops)

    def middle_away(ready, extra):
        def kernel(q_any, k_any, v_any, d_ref, prefix_ref, gq_own_ref, gq_any, gk_ref, gv_ref, *scratch):
            q_ref, k_ref, v_ref, in_sems, gq_ref, out_sems = scratch
            copies = loads(AWAY, (q_any, k_any, v_any), (q_ref, k_ref, v_ref), in_sems)
            for part in copies:
                start(part)
            outs = []

            def give(half, second, source):
                there, here = lay.quarters(half)[second]
                outs.append(pltpu.make_async_copy(source.at[:, here], gq_any.at[:, there], out_sems.at[half, second]))
                outs[-1].start()

            give(OWN, 0, gq_own_ref)
            give(OWN, 1, gq_own_ref)
            mask = causal(rows)
            for second in range(2):
                wait(copies[second])
                for _, _, place, spot in lay.heads(AWAY):
                    if place[0] == second:
                        middle_head(
                            q_ref[:, spot], k_ref[:, spot], v_ref[:, spot], d_ref[:, spot], prefix_ref[spot, :], mask, spot,
                            gq_ref, gk_ref, gv_ref,
                        )
                give(AWAY, second, gq_ref)
            wait(outs)

        args = after(ready, query, key_in, value, d_away, prefix_away, extra["first"][0])
        half_room = pltpu.VMEM((rows, half_wide), BF16)
        scratch = [half_room] * 3 + [pltpu.SemaphoreType.DMA((2, 3)), half_room, pltpu.SemaphoreType.DMA((2, 2))]
        return call(kernel, [whole, wide, wide], args, 5 * block_flops, (0, 1, 2), (0,), scratch)

    beside = {"pair": emit, "first": middle_own, "last": middle_away}
    g_own, g_away, extra = scan(g_keep, g_send, True, beside)
    output = extra["pair"][0]
    grad_q = extra["last"][0]
    near_k = (extra["first"][1], extra["last"][1])
    near_v = (extra["first"][2], extra["last"][2])

    def last(half, suffix, so_far):
        count = 2 * lay.per

        def kernel(k_ref, v_ref, near_k_ref, near_v_ref, *refs):
            suffix_refs = refs[:n]
            gk_any, gv_any, gk_ref, gv_ref, sems = refs[n + len(so_far) :]
            copies = []
            for i, (head, chunk, place, spot) in enumerate(lay.heads(half)):
                cols = columns(head)
                state = suffix_refs[chunk][place].astype(BF16)
                gk_ref[i] = (near_k_ref[:, spot] + dot(v_ref[:, cols], state, ((1,), (1,)))).astype(BF16)
                copies.append(pltpu.make_async_copy(gk_ref.at[i], gk_any.at[:, cols], sems.at[i, 0]))
                copies[-1].start()
                gv_ref[i] = (near_v_ref[:, spot] + dot(k_ref[:, cols], state, ((1,), (0,)))).astype(BF16)
                copies.append(pltpu.make_async_copy(gv_ref.at[i], gv_any.at[:, cols], sems.at[i, 1]))
                copies[-1].start()
            for copy in copies:
                copy.wait()

        args = (key_in, value, near_k[half], near_v[half], *suffix, *so_far)
        first = 4 + n
        return call(
            kernel,
            [whole, whole],
            args,
            2 * state_flops,
            tuple(first + i for i in range(len(so_far))),
            (0, 1),
            [pltpu.VMEM((count, rows, HEAD_DIM), BF16)] * 2 + [pltpu.SemaphoreType.DMA((count, 2))],
            {first + i: i for i in range(len(so_far))},
        )

    grad_k, grad_v = last(AWAY, g_away, tuple(last(OWN, g_own, ())))
    return output, grad_q, grad_k, grad_v


def solution(mesh):
    spec = P("seq", "head")
    return jax.shard_map(local, mesh=mesh, in_specs=(spec,) * 4, out_specs=(spec,) * 4, check_vma=False)
```

```python
import jax
import jax.numpy as jnp
from jax import lax
from jax.experimental import pallas as pl
from jax.experimental.pallas import tpu as pltpu
from jax.sharding import PartitionSpec as P

HEAD_DIM = 128
EPS = 1e-06
F32 = jnp.float32
BF16 = jnp.bfloat16
VMEM = pl.BlockSpec(memory_space=pltpu.VMEM)
HBM = pl.BlockSpec(memory_space=pltpu.HBM)
OWN, AWAY = 0, 1

PIECES = 4


def split(block):
    return block & 1, (block >> 1) & (PIECES - 1), block >> 3


class Half:
    def __init__(self, which, heads):
        core, self.team, _ = split(lax.axis_index("seq"))
        number = core if which == OWN else 1 - core
        self.heads = heads // 2
        self.base = number * (self.heads * HEAD_DIM)
        self.piece_rows = self.heads * HEAD_DIM // PIECES

    def columns(self, start=0, size=None):
        size = self.heads * HEAD_DIM if size is None else size
        return pl.ds(pl.multiple_of(self.base + start, HEAD_DIM), size)

    def state_parts(self, head):
        step = min(self.piece_rows, HEAD_DIM)
        return [
            ((head * HEAD_DIM + row) // self.piece_rows ^ self.team, (head * HEAD_DIM + row) % self.piece_rows, row, step)
            for row in range(0, HEAD_DIM, step)
        ]

    def put(self, ref, head, state):
        for place, there, here, step in self.state_parts(head):
            ref[place, there : there + step, :] = state[here : here + step, :]

    def get(self, ref, head):
        parts = [ref[place, there : there + step, :] for place, there, _, step in self.state_parts(head)]
        return (parts[0] if len(parts) == 1 else jnp.concatenate(parts, axis=0)).astype(BF16)


def dot(a, b, contract):
    return lax.dot_general(a, b, (contract, ((), ())), preferred_element_type=F32)


def causal(rows):
    return lax.broadcasted_iota(jnp.int32, (rows, rows), 0) >= lax.broadcasted_iota(jnp.int32, (rows, rows), 1)


def like(shape, dtype=F32):
    return jax.ShapeDtypeStruct(tuple(shape), dtype)


def call(kernel, outs, args, flops, in_hbm=(), out_hbm=(), scratch=(), alias=None):
    moved = sum(a.size * a.dtype.itemsize for a in (*args, *outs))
    return pl.pallas_call(
        kernel,
        out_shape=outs,
        in_specs=[HBM if i in in_hbm else VMEM for i in range(len(args))],
        out_specs=[HBM if i in out_hbm else VMEM for i in range(len(outs))],
        scratch_shapes=list(scratch),
        input_output_aliases=alias or {},
        cost_estimate=pl.CostEstimate(flops=int(flops), bytes_accessed=int(moved), transcendentals=0),
        compiler_params=pltpu.CompilerParams(vmem_limit_bytes=16 * 1024 * 1024),
    )(*[pltpu.with_memory_space_constraint(a, pltpu.HBM) if i in in_hbm else a for i, a in enumerate(args)])


def exchange(axis, partner, array):
    return lax.ppermute(array, axis, [(i, partner(i)) for i in range(lax.axis_size(axis))])


def after(early, *arrays):
    return lax.optimization_barrier((early, arrays))[1]


def scan(keep, send, reverse, beside):
    count = lax.axis_size("seq")
    core, team, far = split(lax.axis_index("seq"))
    if reverse:
        core, team, far = 1 - core, PIECES - 1 - team, count // 8 - 1 - far
    extra = {}

    def beside_of(name, ready, come):
        if name in beside:
            come, extra[name] = lax.optimization_barrier((come, beside[name](ready, extra)))
        return come

    def to_team(pieces, name):
        come = [exchange("seq", lambda i: i ^ (2 * r), pieces[r]) for r in range(1, PIECES)]
        come[-1] = beside_of(name, pieces[-1], come[-1])
        return [pieces[0], *come]

    got = exchange("seq", lambda i: i ^ 1, send)
    both = keep + got
    edge = lax.optimization_barrier(jnp.where(core == 0, keep, got))
    parts = to_team([both[r] for r in range(PIECES)], "gather")
    total = parts[0] + parts[1] + (parts[2] + parts[3])

    before = jnp.zeros_like(total)
    steps = count // 8
    hop = 1
    while hop < steps:
        if steps & (steps - 1) == 0:
            come = exchange("seq", lambda i: i ^ (8 * hop), total)
            earlier = jnp.where(far & hop != 0, come, 0.0)
        else:
            up = [(i, i + 8 * hop) for i in range(count - 8 * hop)]
            come = lax.ppermute(total, "seq", [(d, s) for s, d in up] if reverse else up)
            earlier = come
        if 2 * hop >= steps:
            come, earlier = beside_of("far", total, (come, earlier))
        before = before + earlier
        total = total + come
        hop *= 2

    starts = []
    for r in range(PIECES):
        start = before
        for other in range(PIECES):
            if other != r:
                start = start + jnp.where((team ^ other) < (team ^ r), parts[other], 0.0)
        starts.append(start)
    base = jnp.stack(to_team(starts, "back"))
    away = exchange("seq", lambda i: i ^ 1, base + jnp.where(core == 0, edge, 0.0))
    own = base + jnp.where(core == 1, edge, 0.0)
    return own, away, extra


def local(query, key_in, value, cotangent):
    rows, width = query.shape
    heads = width // HEAD_DIM
    features = width * lax.axis_size("head")
    half_heads, half_wide = heads // 2, width // 2
    state_flops = heads * rows * HEAD_DIM * HEAD_DIM
    block_flops = heads * rows * rows * HEAD_DIM
    whole = like((rows, width), BF16)
    packed = like((rows, half_wide), BF16)
    wide = like((rows, half_wide))
    states = like((PIECES, half_heads * HEAD_DIM // PIECES, HEAD_DIM))
    spots = [pl.ds(head * HEAD_DIM, HEAD_DIM) for head in range(half_heads)]
    cuts = 2
    cut_heads = half_heads // cuts
    cut_wide = half_wide // cuts

    def loads(half, sources, targets, sems):
        return [
            [
                pltpu.make_async_copy(a.at[:, half.columns(cut * cut_wide, cut_wide)], b.at[:, pl.ds(cut * cut_wide, cut_wide)], sems.at[cut, j])
                for j, (a, b) in enumerate(zip(sources, targets))
            ]
            for cut in range(cuts)
        ]

    def start(copies):
        for copy in copies:
            copy.start()

    def wait(copies):
        for copy in copies:
            copy.wait()

    def first_states(k_any, v_any, k_own_ref, v_own_ref, k_ref, v_ref, out_ref, own_sems, sems):
        half = Half(AWAY, heads)
        near = loads(Half(OWN, heads), (k_any, v_any), (k_own_ref, v_own_ref), own_sems)
        copies = loads(half, (k_any, v_any), (k_ref, v_ref), sems)
        for part in copies + near:
            start(part)
        for head, spot in enumerate(spots):
            if head % cut_heads == 0:
                wait(copies[head // cut_heads])
            half.put(out_ref, head, dot(k_ref[:, spot], v_ref[:, spot], ((0,), (0,))))
        for part in near:
            wait(part)

    k_own, v_own, k_away, v_away, send = call(
        first_states,
        [packed] * 4 + [states],
        (key_in, value),
        state_flops,
        (0, 1),
        (),
        [pltpu.SemaphoreType.DMA((cuts, 2))] * 2,
    )

    def second_states(k_ref, v_ref, out_ref):
        half = Half(OWN, heads)
        for head, spot in enumerate(spots):
            half.put(out_ref, head, dot(k_ref[:, spot], v_ref[:, spot], ((0,), (0,))))

    (keep,) = call(second_states, [states], (k_own, v_own), state_flops)

    def inner(ready, _):
        def kernel(q_ref, *refs):
            mask = causal(rows)
            for which in (OWN, AWAY):
                half = Half(which, heads)
                k_ref, v_ref, near_ref = refs[which], refs[2 + which], refs[4 + which]
                for head, spot in enumerate(spots):
                    q = q_ref[:, half.columns(head * HEAD_DIM, HEAD_DIM)]
                    scores = jnp.where(mask, dot(q, k_ref[:, spot], ((1,), (1,))), 0.0).astype(BF16)
                    near_ref[:, spot] = dot(scores, v_ref[:, spot], ((1,), (0,)))

        args = after(ready, query, k_own, k_away, v_own, v_away)
        return call(kernel, [wide] * 2, args, 4 * block_flops)

    def bring(ready, _):
        def kernel(c_any, own_ref, away_ref, sems):
            copies = [
                pltpu.make_async_copy(c_any.at[:, Half(which, heads).columns()], ref, sems.at[which])
                for which, ref in ((OWN, own_ref), (AWAY, away_ref))
            ]
            start(copies)
            wait(copies)

        return call(kernel, [packed] * 2, after(ready, cotangent), width * rows, (0,), (), [pltpu.SemaphoreType.DMA((2,))])

    own, away, extra = scan(keep, send, False, {"far": inner, "back": bring})
    near, cots = extra["far"], extra["back"]

    def mix(which, prefix):
        def kernel(q_ref, c_ref, near_ref, prefix_ref, mixed_ref, stats_ref, rounded_ref):
            half = Half(which, heads)
            square = jnp.zeros((rows, HEAD_DIM), F32)
            along = jnp.zeros((rows, HEAD_DIM), F32)
            for head, spot in enumerate(spots):
                cols = half.columns(head * HEAD_DIM, HEAD_DIM)
                prefix_b = half.get(prefix_ref, head)
                rounded_ref[spot, :] = prefix_b
                mixed = near_ref[:, spot] + dot(q_ref[:, cols], prefix_b, ((1,), (0,)))
                mixed_ref[:, spot] = mixed
                square += mixed * mixed
                along += c_ref[:, spot].astype(F32) * mixed
            stats_ref[0:1, :] = jnp.sum(square.T, axis=0, keepdims=True)
            stats_ref[1:2, :] = jnp.sum(along.T, axis=0, keepdims=True)

        args = (query, cots[which], near[which], prefix)
        outs = [wide, like((2, rows)), like((half_wide, HEAD_DIM), BF16)]
        return call(kernel, outs, args, state_flops, alias={2: 0})

    mixed_own, stats_own, prefix_own = mix(OWN, own)
    mixed_away, stats_away, prefix_away = mix(AWAY, away)
    mixed = (mixed_own, mixed_away)
    stats = stats_own + stats_away
    if lax.axis_size("head") == 2:
        stats = stats + exchange("head", lambda i: 1 - i, stats)
    else:
        stats = lax.psum(stats, "head")

    def token_scales(stats_ref):
        rstd = lax.rsqrt(stats_ref[0:1, :] / features + EPS)
        slope = rstd * rstd * (stats_ref[1:2, :] / features)
        return (
            jnp.broadcast_to(rstd, (HEAD_DIM, rows)).T,
            jnp.broadcast_to(slope, (HEAD_DIM, rows)).T,
        )

    def grads(which):
        def kernel(q_ref, c_ref, mixed_ref, stats_ref, d_ref, out_ref):
            half = Half(which, heads)
            rstd, slope = token_scales(stats_ref)
            for head, spot in enumerate(spots):
                cols = half.columns(head * HEAD_DIM, HEAD_DIM)
                d_mixed = (rstd * (c_ref[:, spot].astype(F32) - mixed_ref[:, spot] * slope)).astype(BF16)
                d_ref[:, spot] = d_mixed
                half.put(out_ref, head, dot(q_ref[:, cols], d_mixed, ((0,), (0,))))

        return call(kernel, [packed, states], (query, cots[which], mixed[which], stats), state_flops, alias={1: 0})

    d_away, g_send = grads(AWAY)
    d_own, g_keep = grads(OWN)

    def middle_head(q, k, v, d, prefix, mask, spot, gq_ref, gk_ref, gv_ref):
        scores = jnp.where(mask, dot(q, k, ((1,), (1,))), 0.0).astype(BF16)
        d_scores = jnp.where(mask, dot(d, v, ((1,), (1,))), 0.0).astype(BF16)
        gq_ref[:, spot] = (dot(d_scores, k, ((1,), (0,))) + dot(d, prefix, ((1,), (1,)))).astype(BF16)
        gk_ref[:, spot] = dot(d_scores, q, ((0,), (0,))).astype(BF16)
        gv_ref[:, spot] = dot(scores, d, ((0,), (0,))).astype(BF16)

    half_room = pltpu.VMEM((rows, half_wide), BF16)

    def middle_own(ready, _):
        def kernel(
            stats_ref, mixed_own_ref, mixed_away_ref, d_ref, prefix_ref, q_any, k_any, v_any,
            out_any, gq_ref, gk_ref, gv_ref, q_ref, k_ref, v_ref, in_sems, out_own_ref, out_away_ref, out_sems,
        ):
            half = Half(OWN, heads)
            copies = loads(half, (q_any, k_any, v_any), (q_ref, k_ref, v_ref), in_sems)
            for part in copies:
                start(part)
            rstd, _ = token_scales(stats_ref)
            outs = []
            for which, mixed_ref, out_ref in ((OWN, mixed_own_ref, out_own_ref), (AWAY, mixed_away_ref, out_away_ref)):
                for spot in spots:
                    out_ref[:, spot] = (mixed_ref[:, spot] * rstd).astype(BF16)
                there = out_any.at[:, Half(which, heads).columns()]
                outs.append(pltpu.make_async_copy(out_ref, there, out_sems.at[which]))
                outs[-1].start()
            mask = causal(rows)
            for head, spot in enumerate(spots):
                if head % cut_heads == 0:
                    wait(copies[head // cut_heads])
                middle_head(
                    q_ref[:, spot], k_ref[:, spot], v_ref[:, spot], d_ref[:, spot], prefix_ref[spot, :], mask, spot,
                    gq_ref, gk_ref, gv_ref,
                )
            wait(outs)

        args = after(ready, stats, *mixed, d_own, prefix_own, query, key_in, value)
        scratch = [half_room] * 3 + [pltpu.SemaphoreType.DMA((cuts, 3))] + [half_room] * 2 + [pltpu.SemaphoreType.DMA((2,))]
        return call(kernel, [whole, packed, packed, packed], args, 5 * block_flops, (5, 6, 7), (0,), scratch, {3: 1})

    def middle_away(ready, _):
        def kernel(d_ref, prefix_ref, q_any, k_any, v_any, gq_ref, gk_ref, gv_ref, q_ref, k_ref, v_ref, in_sems):
            copies = loads(Half(AWAY, heads), (q_any, k_any, v_any), (q_ref, k_ref, v_ref), in_sems)
            for part in copies:
                start(part)
            mask = causal(rows)
            for head, spot in enumerate(spots):
                if head % cut_heads == 0:
                    wait(copies[head // cut_heads])
                middle_head(
                    q_ref[:, spot], k_ref[:, spot], v_ref[:, spot], d_ref[:, spot], prefix_ref[spot, :], mask, spot,
                    gq_ref, gk_ref, gv_ref,
                )

        args = after(ready, d_away, prefix_away, query, key_in, value)
        scratch = [half_room] * 3 + [pltpu.SemaphoreType.DMA((cuts, 3))]
        return call(kernel, [packed] * 3, args, 5 * block_flops, (2, 3, 4), (), scratch, {0: 0})

    def turn(ready, extra):
        def kernel(own_ref, away_ref, k_any, v_any, out_any, k_own_ref, v_own_ref, k_away_ref, v_away_ref, sems):
            copies = []
            for which, ref, k_ref, v_ref in ((OWN, own_ref, k_own_ref, v_own_ref), (AWAY, away_ref, k_away_ref, v_away_ref)):
                cols = Half(which, heads).columns()
                copies.append(pltpu.make_async_copy(k_any.at[:, cols], k_ref, sems.at[which, 0]))
                copies.append(pltpu.make_async_copy(v_any.at[:, cols], v_ref, sems.at[which, 1]))
                copies.append(pltpu.make_async_copy(ref, out_any.at[:, cols], sems.at[which, 2]))
            start(copies)
            wait(copies)

        args = after(ready, extra["gather"][1], extra["far"][0], key_in, value)
        scratch = [pltpu.SemaphoreType.DMA((2, 3))]
        return call(kernel, [whole] + [packed] * 4, args, width * rows, (2, 3), (0,), scratch)

    beside = {"gather": middle_own, "far": middle_away, "back": turn}
    g_own, g_away, extra = scan(g_keep, g_send, True, beside)
    output, _, *near_own = extra["gather"]
    _, *near_away = extra["far"]
    grad_q, *known = extra["back"]

    def last(which, suffix, so_far):
        def kernel(k_ref, v_ref, near_k_ref, near_v_ref, suffix_ref, *refs):
            gk_any, gv_any, gk_ref, gv_ref, sems = refs[len(so_far) :]
            half = Half(which, heads)
            copies = []
            for head, spot in enumerate(spots):
                state = half.get(suffix_ref, head)
                gk_ref[:, spot] = (near_k_ref[:, spot] + dot(v_ref[:, spot], state, ((1,), (1,)))).astype(BF16)
                gv_ref[:, spot] = (near_v_ref[:, spot] + dot(k_ref[:, spot], state, ((1,), (0,)))).astype(BF16)
                if (head + 1) % cut_heads == 0:
                    cut = head // cut_heads
                    here = pl.ds(cut * cut_wide, cut_wide)
                    there = half.columns(cut * cut_wide, cut_wide)
                    for j, (ref, out) in enumerate(((gk_ref, gk_any), (gv_ref, gv_any))):
                        copies.append(pltpu.make_async_copy(ref.at[:, here], out.at[:, there], sems.at[cut, j]))
                        copies[-1].start()
            wait(copies)

        args = (*known[2 * which : 2 * which + 2], *(near_own, near_away)[which], suffix, *so_far)
        return call(
            kernel,
            [whole, whole],
            args,
            2 * state_flops,
            tuple(5 + i for i in range(len(so_far))),
            (0, 1),
            [pltpu.VMEM((rows, half_wide), BF16)] * 2 + [pltpu.SemaphoreType.DMA((cuts, 2))],
            {5 + i: i for i in range(len(so_far))},
        )

    grad_k, grad_v = last(AWAY, g_away, tuple(last(OWN, g_own, ())))
    return output, grad_q, grad_k, grad_v


def solution(mesh):
    spec = P("seq", "head")
    return jax.shard_map(local, mesh=mesh, in_specs=(spec,) * 4, out_specs=(spec,) * 4, check_vma=False)
```

```python
import jax
import jax.numpy as jnp
from jax import lax
from jax.experimental import pallas as pl
from jax.experimental.pallas import tpu as pltpu
from jax.sharding import PartitionSpec as P

HEAD_DIM = 128
EPS = 1e-06
F32 = jnp.float32
BF16 = jnp.bfloat16
VMEM = pl.BlockSpec(memory_space=pltpu.VMEM)
HBM = pl.BlockSpec(memory_space=pltpu.HBM)
OWN, AWAY = 0, 1

PIECES = 4
ORDER = (2, 1, 3)


def crosses(bits):
    return (bits & 1) ^ (bits >> 1)


def split(block):
    return block & 1, (block >> 1) & (PIECES - 1), block >> 3


class Half:
    def __init__(self, which, heads):
        core, self.team, _ = split(lax.axis_index("seq"))
        own = core ^ crosses(self.team)
        number = own if which == OWN else 1 - own
        self.heads = heads // 2
        self.base = number * (self.heads * HEAD_DIM)
        self.piece_rows = self.heads * HEAD_DIM // PIECES

    def columns(self, start=0, size=None):
        size = self.heads * HEAD_DIM if size is None else size
        return pl.ds(pl.multiple_of(self.base + start, HEAD_DIM), size)

    def state_parts(self, head):
        step = min(self.piece_rows, HEAD_DIM)
        return [
            ((head * HEAD_DIM + row) // self.piece_rows ^ self.team, (head * HEAD_DIM + row) % self.piece_rows, row, step)
            for row in range(0, HEAD_DIM, step)
        ]

    def put(self, ref, head, state):
        for place, there, here, step in self.state_parts(head):
            ref[place, there : there + step, :] = state[here : here + step, :]

    def get(self, ref, head):
        parts = [ref[place, there : there + step, :] for place, there, _, step in self.state_parts(head)]
        return (parts[0] if len(parts) == 1 else jnp.concatenate(parts, axis=0)).astype(BF16)


def dot(a, b, contract):
    return lax.dot_general(a, b, (contract, ((), ())), preferred_element_type=F32)


def causal(rows):
    return lax.broadcasted_iota(jnp.int32, (rows, rows), 0) >= lax.broadcasted_iota(jnp.int32, (rows, rows), 1)


def like(shape, dtype=F32):
    return jax.ShapeDtypeStruct(tuple(shape), dtype)


def call(kernel, outs, args, flops, in_hbm=(), out_hbm=(), scratch=(), alias=None):
    moved = sum(a.size * a.dtype.itemsize for a in (*args, *outs))
    return pl.pallas_call(
        kernel,
        out_shape=outs,
        in_specs=[HBM if i in in_hbm else VMEM for i in range(len(args))],
        out_specs=[HBM if i in out_hbm else VMEM for i in range(len(outs))],
        scratch_shapes=list(scratch),
        input_output_aliases=alias or {},
        cost_estimate=pl.CostEstimate(flops=int(flops), bytes_accessed=int(moved), transcendentals=0),
        compiler_params=pltpu.CompilerParams(vmem_limit_bytes=16 * 1024 * 1024),
    )(*[pltpu.with_memory_space_constraint(a, pltpu.HBM) if i in in_hbm else a for i, a in enumerate(args)])


def exchange(axis, partner, array):
    return lax.ppermute(array, axis, [(i, partner(i)) for i in range(lax.axis_size(axis))])


def after(early, *arrays):
    return lax.optimization_barrier((early, arrays))[1]


def scan(keep, send, reverse, beside):
    count = lax.axis_size("seq")
    core, team, far = split(lax.axis_index("seq"))
    if reverse:
        core, team, far = 1 - core, PIECES - 1 - team, count // 8 - 1 - far
    extra = {}

    def beside_of(name, ready, come):
        if name in beside:
            come, extra[name] = lax.optimization_barrier((come, beside[name](ready, extra)))
        return come

    def to_team(pieces, name):
        come = {0: pieces[0]}
        for r in ORDER:
            come[r] = exchange("seq", lambda i: i ^ (2 * r) ^ crosses(r), pieces[r])
        come[r] = beside_of(name, pieces[r], come[r])
        return [come[r] for r in range(PIECES)]

    got = exchange("seq", lambda i: i ^ 1, send)
    both = keep + got
    edge = lax.optimization_barrier(jnp.where(core == 0, keep, got))
    parts = to_team([both[r] for r in range(PIECES)], "gather")
    total = parts[0] + parts[1] + (parts[2] + parts[3])

    before = jnp.zeros_like(total)
    steps = count // 8
    hop = 1
    while hop < steps:
        if steps & (steps - 1) == 0:
            come = exchange("seq", lambda i: i ^ (8 * hop), total)
            earlier = jnp.where(far & hop != 0, come, 0.0)
        else:
            up = [(i, i + 8 * hop) for i in range(count - 8 * hop)]
            come = lax.ppermute(total, "seq", [(d, s) for s, d in up] if reverse else up)
            earlier = come
        if 2 * hop >= steps:
            come, earlier = beside_of("far", total, (come, earlier))
        before = before + earlier
        total = total + come
        hop *= 2

    starts = []
    for r in range(PIECES):
        start = before
        for other in range(PIECES):
            if other != r:
                start = start + jnp.where((team ^ other) < (team ^ r), parts[other], 0.0)
        starts.append(start)
    base = jnp.stack(to_team(starts, "back"))
    away = exchange("seq", lambda i: i ^ 1, base + jnp.where(core == 0, edge, 0.0))
    own = base + jnp.where(core == 1, edge, 0.0)
    return own, away, extra


def local(query, key_in, value, cotangent):
    rows, width = query.shape
    heads = width // HEAD_DIM
    features = width * lax.axis_size("head")
    half_heads, half_wide = heads // 2, width // 2
    state_flops = heads * rows * HEAD_DIM * HEAD_DIM
    block_flops = heads * rows * rows * HEAD_DIM
    whole = like((rows, width), BF16)
    packed = like((rows, half_wide), BF16)
    wide = like((rows, half_wide))
    states = like((PIECES, half_heads * HEAD_DIM // PIECES, HEAD_DIM))
    spots = [pl.ds(head * HEAD_DIM, HEAD_DIM) for head in range(half_heads)]
    cuts = 2
    cut_heads = half_heads // cuts
    cut_wide = half_wide // cuts

    def loads(half, sources, targets, sems):
        return [
            [
                pltpu.make_async_copy(a.at[:, half.columns(cut * cut_wide, cut_wide)], b.at[:, pl.ds(cut * cut_wide, cut_wide)], sems.at[cut, j])
                for j, (a, b) in enumerate(zip(sources, targets))
            ]
            for cut in range(cuts)
        ]

    def start(copies):
        for copy in copies:
            copy.start()

    def wait(copies):
        for copy in copies:
            copy.wait()

    def first_states(k_any, v_any, k_own_ref, v_own_ref, k_ref, v_ref, out_ref, own_sems, sems):
        half = Half(AWAY, heads)
        near = loads(Half(OWN, heads), (k_any, v_any), (k_own_ref, v_own_ref), own_sems)
        copies = loads(half, (k_any, v_any), (k_ref, v_ref), sems)
        for part in copies + near:
            start(part)
        for head, spot in enumerate(spots):
            if head % cut_heads == 0:
                wait(copies[head // cut_heads])
            half.put(out_ref, head, dot(k_ref[:, spot], v_ref[:, spot], ((0,), (0,))))
        for part in near:
            wait(part)

    k_own, v_own, k_away, v_away, send = call(
        first_states,
        [packed] * 4 + [states],
        (key_in, value),
        state_flops,
        (0, 1),
        (),
        [pltpu.SemaphoreType.DMA((cuts, 2))] * 2,
    )

    def second_states(k_ref, v_ref, out_ref):
        half = Half(OWN, heads)
        for head, spot in enumerate(spots):
            half.put(out_ref, head, dot(k_ref[:, spot], v_ref[:, spot], ((0,), (0,))))

    (keep,) = call(second_states, [states], (k_own, v_own), state_flops)

    def inner(ready, _):
        def kernel(q_ref, *refs):
            mask = causal(rows)
            for which in (OWN, AWAY):
                half = Half(which, heads)
                k_ref, v_ref, near_ref = refs[which], refs[2 + which], refs[4 + which]
                for head, spot in enumerate(spots):
                    q = q_ref[:, half.columns(head * HEAD_DIM, HEAD_DIM)]
                    scores = jnp.where(mask, dot(q, k_ref[:, spot], ((1,), (1,))), 0.0).astype(BF16)
                    near_ref[:, spot] = dot(scores, v_ref[:, spot], ((1,), (0,)))

        args = after(ready, query, k_own, k_away, v_own, v_away)
        return call(kernel, [wide] * 2, args, 4 * block_flops)

    def bring(ready, _):
        def kernel(c_any, own_ref, away_ref, sems):
            copies = [
                pltpu.make_async_copy(c_any.at[:, Half(which, heads).columns()], ref, sems.at[which])
                for which, ref in ((OWN, own_ref), (AWAY, away_ref))
            ]
            start(copies)
            wait(copies)

        return call(kernel, [packed] * 2, after(ready, cotangent), width * rows, (0,), (), [pltpu.SemaphoreType.DMA((2,))])

    own, away, extra = scan(keep, send, False, {"far": inner, "back": bring})
    near, cots = extra["far"], extra["back"]

    def mix(which, prefix):
        def kernel(q_ref, c_ref, near_ref, prefix_ref, mixed_ref, stats_ref, rounded_ref):
            half = Half(which, heads)
            square = jnp.zeros((rows, HEAD_DIM), F32)
            along = jnp.zeros((rows, HEAD_DIM), F32)
            for head, spot in enumerate(spots):
                cols = half.columns(head * HEAD_DIM, HEAD_DIM)
                prefix_b = half.get(prefix_ref, head)
                rounded_ref[spot, :] = prefix_b
                mixed = near_ref[:, spot] + dot(q_ref[:, cols], prefix_b, ((1,), (0,)))
                mixed_ref[:, spot] = mixed
                square += mixed * mixed
                along += c_ref[:, spot].astype(F32) * mixed
            stats_ref[0:1, :] = jnp.sum(square.T, axis=0, keepdims=True)
            stats_ref[1:2, :] = jnp.sum(along.T, axis=0, keepdims=True)

        args = (query, cots[which], near[which], prefix)
        outs = [wide, like((2, rows)), like((half_wide, HEAD_DIM), BF16)]
        return call(kernel, outs, args, state_flops, alias={2: 0})

    mixed_own, stats_own, prefix_own = mix(OWN, own)
    mixed_away, stats_away, prefix_away = mix(AWAY, away)
    mixed = (mixed_own, mixed_away)
    stats = stats_own + stats_away
    if lax.axis_size("head") == 2:
        stats = stats + exchange("head", lambda i: 1 - i, stats)
    else:
        stats = lax.psum(stats, "head")

    def token_scales(stats_ref):
        rstd = lax.rsqrt(stats_ref[0:1, :] / features + EPS)
        slope = rstd * rstd * (stats_ref[1:2, :] / features)
        return (
            jnp.broadcast_to(rstd, (HEAD_DIM, rows)).T,
            jnp.broadcast_to(slope, (HEAD_DIM, rows)).T,
        )

    def grads(which):
        def kernel(q_ref, c_ref, mixed_ref, stats_ref, d_ref, out_ref):
            half = Half(which, heads)
            rstd, slope = token_scales(stats_ref)
            for head, spot in enumerate(spots):
                cols = half.columns(head * HEAD_DIM, HEAD_DIM)
                d_mixed = (rstd * (c_ref[:, spot].astype(F32) - mixed_ref[:, spot] * slope)).astype(BF16)
                d_ref[:, spot] = d_mixed
                half.put(out_ref, head, dot(q_ref[:, cols], d_mixed, ((0,), (0,))))

        return call(kernel, [packed, states], (query, cots[which], mixed[which], stats), state_flops, alias={1: 0})

    d_away, g_send = grads(AWAY)
    d_own, g_keep = grads(OWN)

    def middle_head(q, k, v, d, prefix, mask, spot, gq_ref, gk_ref, gv_ref):
        scores = jnp.where(mask, dot(q, k, ((1,), (1,))), 0.0).astype(BF16)
        d_scores = jnp.where(mask, dot(d, v, ((1,), (1,))), 0.0).astype(BF16)
        gq_ref[:, spot] = (dot(d_scores, k, ((1,), (0,))) + dot(d, prefix, ((1,), (1,)))).astype(BF16)
        gk_ref[:, spot] = dot(d_scores, q, ((0,), (0,))).astype(BF16)
        gv_ref[:, spot] = dot(scores, d, ((0,), (0,))).astype(BF16)

    half_room = pltpu.VMEM((rows, half_wide), BF16)

    def middle_own(ready, _):
        def kernel(
            stats_ref, mixed_own_ref, mixed_away_ref, d_ref, prefix_ref, q_any, k_any, v_any,
            out_any, gq_ref, gk_ref, gv_ref, q_ref, k_ref, v_ref, in_sems, out_own_ref, out_away_ref, out_sems,
        ):
            half = Half(OWN, heads)
            copies = loads(half, (q_any, k_any, v_any), (q_ref, k_ref, v_ref), in_sems)
            for part in copies:
                start(part)
            rstd, _ = token_scales(stats_ref)
            outs = []
            for which, mixed_ref, out_ref in ((OWN, mixed_own_ref, out_own_ref), (AWAY, mixed_away_ref, out_away_ref)):
                for spot in spots:
                    out_ref[:, spot] = (mixed_ref[:, spot] * rstd).astype(BF16)
                there = out_any.at[:, Half(which, heads).columns()]
                outs.append(pltpu.make_async_copy(out_ref, there, out_sems.at[which]))
                outs[-1].start()
            mask = causal(rows)
            for head, spot in enumerate(spots):
                if head % cut_heads == 0:
                    wait(copies[head // cut_heads])
                middle_head(
                    q_ref[:, spot], k_ref[:, spot], v_ref[:, spot], d_ref[:, spot], prefix_ref[spot, :], mask, spot,
                    gq_ref, gk_ref, gv_ref,
                )
            wait(outs)

        args = after(ready, stats, *mixed, d_own, prefix_own, query, key_in, value)
        scratch = [half_room] * 3 + [pltpu.SemaphoreType.DMA((cuts, 3))] + [half_room] * 2 + [pltpu.SemaphoreType.DMA((2,))]
        return call(kernel, [whole, packed, packed, packed], args, 5 * block_flops, (5, 6, 7), (0,), scratch, {3: 1})

    def middle_away(ready, _):
        def kernel(d_ref, prefix_ref, q_any, k_any, v_any, gq_ref, gk_ref, gv_ref, q_ref, k_ref, v_ref, in_sems):
            copies = loads(Half(AWAY, heads), (q_any, k_any, v_any), (q_ref, k_ref, v_ref), in_sems)
            for part in copies:
                start(part)
            mask = causal(rows)
            for head, spot in enumerate(spots):
                if head % cut_heads == 0:
                    wait(copies[head // cut_heads])
                middle_head(
                    q_ref[:, spot], k_ref[:, spot], v_ref[:, spot], d_ref[:, spot], prefix_ref[spot, :], mask, spot,
                    gq_ref, gk_ref, gv_ref,
                )

        args = after(ready, d_away, prefix_away, query, key_in, value)
        scratch = [half_room] * 3 + [pltpu.SemaphoreType.DMA((cuts, 3))]
        return call(kernel, [packed] * 3, args, 5 * block_flops, (2, 3, 4), (), scratch, {0: 0})

    def turn(ready, extra):
        def kernel(own_ref, away_ref, k_any, v_any, out_any, k_own_ref, v_own_ref, k_away_ref, v_away_ref, sems):
            copies = []
            for which, ref, k_ref, v_ref in ((OWN, own_ref, k_own_ref, v_own_ref), (AWAY, away_ref, k_away_ref, v_away_ref)):
                cols = Half(which, heads).columns()
                copies.append(pltpu.make_async_copy(k_any.at[:, cols], k_ref, sems.at[which, 0]))
                copies.append(pltpu.make_async_copy(v_any.at[:, cols], v_ref, sems.at[which, 1]))
                copies.append(pltpu.make_async_copy(ref, out_any.at[:, cols], sems.at[which, 2]))
            start(copies)
            wait(copies)

        args = after(ready, extra["gather"][1], extra["far"][0], key_in, value)
        scratch = [pltpu.SemaphoreType.DMA((2, 3))]
        return call(kernel, [whole] + [packed] * 4, args, width * rows, (2, 3), (0,), scratch)

    beside = {"gather": middle_own, "far": middle_away, "back": turn}
    g_own, g_away, extra = scan(g_keep, g_send, True, beside)
    output, _, *near_own = extra["gather"]
    _, *near_away = extra["far"]
    grad_q, *known = extra["back"]

    def last(which, suffix, so_far):
        def kernel(k_ref, v_ref, near_k_ref, near_v_ref, suffix_ref, *refs):
            gk_any, gv_any, gk_ref, gv_ref, sems = refs[len(so_far) :]
            half = Half(which, heads)
            copies = []
            for head, spot in enumerate(spots):
                state = half.get(suffix_ref, head)
                gk_ref[:, spot] = (near_k_ref[:, spot] + dot(v_ref[:, spot], state, ((1,), (1,)))).astype(BF16)
                gv_ref[:, spot] = (near_v_ref[:, spot] + dot(k_ref[:, spot], state, ((1,), (0,)))).astype(BF16)
                if (head + 1) % cut_heads == 0:
                    cut = head // cut_heads
                    here = pl.ds(cut * cut_wide, cut_wide)
                    there = half.columns(cut * cut_wide, cut_wide)
                    for j, (ref, out) in enumerate(((gk_ref, gk_any), (gv_ref, gv_any))):
                        copies.append(pltpu.make_async_copy(ref.at[:, here], out.at[:, there], sems.at[cut, j]))
                        copies[-1].start()
            wait(copies)

        args = (*known[2 * which : 2 * which + 2], *(near_own, near_away)[which], suffix, *so_far)
        return call(
            kernel,
            [whole, whole],
            args,
            2 * state_flops,
            tuple(5 + i for i in range(len(so_far))),
            (0, 1),
            [pltpu.VMEM((rows, half_wide), BF16)] * 2 + [pltpu.SemaphoreType.DMA((cuts, 2))],
            {5 + i: i for i in range(len(so_far))},
        )

    grad_k, grad_v = last(AWAY, g_away, tuple(last(OWN, g_own, ())))
    return output, grad_q, grad_k, grad_v


def solution(mesh):
    spec = P("seq", "head")
    return jax.shard_map(local, mesh=mesh, in_specs=(spec,) * 4, out_specs=(spec,) * 4, check_vma=False)
```

```python
import jax
import jax.numpy as jnp
from jax import lax
from jax.experimental import pallas as pl
from jax.experimental.pallas import tpu as pltpu
from jax.sharding import PartitionSpec as P

HEAD_DIM = 128
EPS = 1e-06
F32 = jnp.float32
BF16 = jnp.bfloat16
VMEM = pl.BlockSpec(memory_space=pltpu.VMEM)
HBM = pl.BlockSpec(memory_space=pltpu.HBM)
OWN, AWAY = 0, 1

PIECES = 4
ORDER = {"gather": (1, 2, 3), "back": (2, 1, 3)}


def crosses(bits):
    return (bits & 1) ^ (bits >> 1)


def split(block):
    return block & 1, (block >> 1) & (PIECES - 1), block >> 3


class Half:
    def __init__(self, which, heads):
        core, self.team, _ = split(lax.axis_index("seq"))
        own = core ^ crosses(self.team)
        number = own if which == OWN else 1 - own
        self.heads = heads // 2
        self.base = number * (self.heads * HEAD_DIM)
        self.piece_rows = self.heads * HEAD_DIM // PIECES

    def columns(self, start=0, size=None):
        size = self.heads * HEAD_DIM if size is None else size
        return pl.ds(pl.multiple_of(self.base + start, HEAD_DIM), size)

    def state_parts(self, head):
        step = min(self.piece_rows, HEAD_DIM)
        return [
            ((head * HEAD_DIM + row) // self.piece_rows ^ self.team, (head * HEAD_DIM + row) % self.piece_rows, row, step)
            for row in range(0, HEAD_DIM, step)
        ]

    def put(self, ref, head, state):
        for place, there, here, step in self.state_parts(head):
            ref[place, there : there + step, :] = state[here : here + step, :]

    def get(self, ref, head):
        parts = [ref[place, there : there + step, :] for place, there, _, step in self.state_parts(head)]
        return (parts[0] if len(parts) == 1 else jnp.concatenate(parts, axis=0)).astype(BF16)


def dot(a, b, contract):
    return lax.dot_general(a, b, (contract, ((), ())), preferred_element_type=F32)


def causal(rows):
    return lax.broadcasted_iota(jnp.int32, (rows, rows), 0) >= lax.broadcasted_iota(jnp.int32, (rows, rows), 1)


def like(shape, dtype=F32):
    return jax.ShapeDtypeStruct(tuple(shape), dtype)


def call(kernel, outs, args, flops, in_hbm=(), out_hbm=(), scratch=(), alias=None):
    moved = sum(a.size * a.dtype.itemsize for a in (*args, *outs))
    return pl.pallas_call(
        kernel,
        out_shape=outs,
        in_specs=[HBM if i in in_hbm else VMEM for i in range(len(args))],
        out_specs=[HBM if i in out_hbm else VMEM for i in range(len(outs))],
        scratch_shapes=list(scratch),
        input_output_aliases=alias or {},
        cost_estimate=pl.CostEstimate(flops=int(flops), bytes_accessed=int(moved), transcendentals=0),
        compiler_params=pltpu.CompilerParams(vmem_limit_bytes=16 * 1024 * 1024),
    )(*[pltpu.with_memory_space_constraint(a, pltpu.HBM) if i in in_hbm else a for i, a in enumerate(args)])


def exchange(axis, partner, array):
    return lax.ppermute(array, axis, [(i, partner(i)) for i in range(lax.axis_size(axis))])


def after(early, *arrays):
    return lax.optimization_barrier((early, arrays))[1]


def scan(keep, send, reverse, beside):
    count = lax.axis_size("seq")
    core, team, far = split(lax.axis_index("seq"))
    if reverse:
        core, team, far = 1 - core, PIECES - 1 - team, count // 8 - 1 - far
    extra = {}

    def beside_of(name, ready, come):
        if name in beside:
            come, extra[name] = lax.optimization_barrier((come, beside[name](ready, extra)))
        return come

    def to_team(pieces, name):
        come = {0: pieces[0]}
        for r in ORDER[name]:
            come[r] = exchange("seq", lambda i: i ^ (2 * r) ^ crosses(r), pieces[r])
        come[r] = beside_of(name, pieces[r], come[r])
        return [come[r] for r in range(PIECES)]

    got = exchange("seq", lambda i: i ^ 1, send)
    both = keep + got
    edge = lax.optimization_barrier(jnp.where(core == 0, keep, got))
    parts = to_team([both[r] for r in range(PIECES)], "gather")
    total = parts[0] + parts[1] + (parts[2] + parts[3])

    before = jnp.zeros_like(total)
    steps = count // 8
    hop = 1
    while hop < steps:
        if steps & (steps - 1) == 0:
            come = exchange("seq", lambda i: i ^ (8 * hop), total)
            earlier = jnp.where(far & hop != 0, come, 0.0)
        else:
            up = [(i, i + 8 * hop) for i in range(count - 8 * hop)]
            come = lax.ppermute(total, "seq", [(d, s) for s, d in up] if reverse else up)
            earlier = come
        if 2 * hop >= steps:
            come, earlier = beside_of("far", total, (come, earlier))
        before = before + earlier
        total = total + come
        hop *= 2

    starts = []
    for r in range(PIECES):
        start = before
        for other in range(PIECES):
            if other != r:
                start = start + jnp.where((team ^ other) < (team ^ r), parts[other], 0.0)
        starts.append(start)
    base = jnp.stack(to_team(starts, "back"))
    away = exchange("seq", lambda i: i ^ 1, base + jnp.where(core == 0, edge, 0.0))
    own = base + jnp.where(core == 1, edge, 0.0)
    return own, away, extra


def local(query, key_in, value, cotangent):
    rows, width = query.shape
    heads = width // HEAD_DIM
    features = width * lax.axis_size("head")
    half_heads, half_wide = heads // 2, width // 2
    state_flops = heads * rows * HEAD_DIM * HEAD_DIM
    block_flops = heads * rows * rows * HEAD_DIM
    whole = like((rows, width), BF16)
    packed = like((rows, half_wide), BF16)
    wide = like((rows, half_wide))
    states = like((PIECES, half_heads * HEAD_DIM // PIECES, HEAD_DIM))
    spots = [pl.ds(head * HEAD_DIM, HEAD_DIM) for head in range(half_heads)]
    cuts = 1
    cut_heads = half_heads // cuts
    cut_wide = half_wide // cuts

    def loads(half, sources, targets, sems):
        return [
            [
                pltpu.make_async_copy(a.at[:, half.columns(cut * cut_wide, cut_wide)], b.at[:, pl.ds(cut * cut_wide, cut_wide)], sems.at[cut, j])
                for j, (a, b) in enumerate(zip(sources, targets))
            ]
            for cut in range(cuts)
        ]

    def start(copies):
        for copy in copies:
            copy.start()

    def wait(copies):
        for copy in copies:
            copy.wait()

    def first_states(k_any, v_any, k_own_ref, v_own_ref, k_ref, v_ref, out_ref, own_sems, sems):
        half = Half(AWAY, heads)
        near = loads(Half(OWN, heads), (k_any, v_any), (k_own_ref, v_own_ref), own_sems)
        copies = loads(half, (k_any, v_any), (k_ref, v_ref), sems)
        for part in copies + near:
            start(part)
        for head, spot in enumerate(spots):
            if head % cut_heads == 0:
                wait(copies[head // cut_heads])
            half.put(out_ref, head, dot(k_ref[:, spot], v_ref[:, spot], ((0,), (0,))))
        for part in near:
            wait(part)

    k_own, v_own, k_away, v_away, send = call(
        first_states,
        [packed] * 4 + [states],
        (key_in, value),
        state_flops,
        (0, 1),
        (),
        [pltpu.SemaphoreType.DMA((cuts, 2))] * 2,
    )

    def second_states(k_ref, v_ref, out_ref):
        half = Half(OWN, heads)
        for head, spot in enumerate(spots):
            half.put(out_ref, head, dot(k_ref[:, spot], v_ref[:, spot], ((0,), (0,))))

    (keep,) = call(second_states, [states], (k_own, v_own), state_flops)

    def inner(ready, _):
        def kernel(q_ref, *refs):
            mask = causal(rows)
            for which in (OWN, AWAY):
                half = Half(which, heads)
                k_ref, v_ref, near_ref = refs[which], refs[2 + which], refs[4 + which]
                for head, spot in enumerate(spots):
                    q = q_ref[:, half.columns(head * HEAD_DIM, HEAD_DIM)]
                    scores = jnp.where(mask, dot(q, k_ref[:, spot], ((1,), (1,))), 0.0).astype(BF16)
                    near_ref[:, spot] = dot(scores, v_ref[:, spot], ((1,), (0,)))

        args = after(ready, query, k_own, k_away, v_own, v_away)
        return call(kernel, [wide] * 2, args, 4 * block_flops)

    def bring(ready, _):
        def kernel(c_any, own_ref, away_ref, sems):
            copies = [
                pltpu.make_async_copy(c_any.at[:, Half(which, heads).columns()], ref, sems.at[which])
                for which, ref in ((OWN, own_ref), (AWAY, away_ref))
            ]
            start(copies)
            wait(copies)

        return call(kernel, [packed] * 2, after(ready, cotangent), width * rows, (0,), (), [pltpu.SemaphoreType.DMA((2,))])

    own, away, extra = scan(keep, send, False, {"far": inner, "back": bring})
    near, cots = extra["far"], extra["back"]

    def mix(which, prefix):
        def kernel(q_ref, c_ref, near_ref, prefix_ref, mixed_ref, stats_ref, rounded_ref):
            half = Half(which, heads)
            square = jnp.zeros((rows, HEAD_DIM), F32)
            along = jnp.zeros((rows, HEAD_DIM), F32)
            for head, spot in enumerate(spots):
                cols = half.columns(head * HEAD_DIM, HEAD_DIM)
                prefix_b = half.get(prefix_ref, head)
                rounded_ref[spot, :] = prefix_b
                mixed = near_ref[:, spot] + dot(q_ref[:, cols], prefix_b, ((1,), (0,)))
                mixed_ref[:, spot] = mixed
                square += mixed * mixed
                along += c_ref[:, spot].astype(F32) * mixed
            stats_ref[0:1, :] = jnp.sum(square.T, axis=0, keepdims=True)
            stats_ref[1:2, :] = jnp.sum(along.T, axis=0, keepdims=True)

        args = (query, cots[which], near[which], prefix)
        outs = [wide, like((2, rows)), like((half_wide, HEAD_DIM), BF16)]
        return call(kernel, outs, args, state_flops, alias={2: 0})

    mixed_own, stats_own, prefix_own = mix(OWN, own)
    mixed_away, stats_away, prefix_away = mix(AWAY, away)
    mixed = (mixed_own, mixed_away)
    stats = stats_own + stats_away
    if lax.axis_size("head") == 2:
        stats = stats + exchange("head", lambda i: 1 - i, stats)
    else:
        stats = lax.psum(stats, "head")

    def token_scales(stats_ref):
        rstd = lax.rsqrt(stats_ref[0:1, :] / features + EPS)
        slope = rstd * rstd * (stats_ref[1:2, :] / features)
        return (
            jnp.broadcast_to(rstd, (HEAD_DIM, rows)).T,
            jnp.broadcast_to(slope, (HEAD_DIM, rows)).T,
        )

    def grads(which):
        def kernel(q_ref, c_ref, mixed_ref, stats_ref, d_ref, out_ref):
            half = Half(which, heads)
            rstd, slope = token_scales(stats_ref)
            for head, spot in enumerate(spots):
                cols = half.columns(head * HEAD_DIM, HEAD_DIM)
                d_mixed = (rstd * (c_ref[:, spot].astype(F32) - mixed_ref[:, spot] * slope)).astype(BF16)
                d_ref[:, spot] = d_mixed
                half.put(out_ref, head, dot(q_ref[:, cols], d_mixed, ((0,), (0,))))

        return call(kernel, [packed, states], (query, cots[which], mixed[which], stats), state_flops, alias={1: 0})

    d_away, g_send = grads(AWAY)
    d_own, g_keep = grads(OWN)

    def middle_head(q, k, v, d, prefix, mask, spot, gq_ref, gk_ref, gv_ref):
        scores = jnp.where(mask, dot(q, k, ((1,), (1,))), 0.0).astype(BF16)
        d_scores = jnp.where(mask, dot(d, v, ((1,), (1,))), 0.0).astype(BF16)
        gq_ref[:, spot] = (dot(d_scores, k, ((1,), (0,))) + dot(d, prefix, ((1,), (1,)))).astype(BF16)
        gk_ref[:, spot] = dot(d_scores, q, ((0,), (0,))).astype(BF16)
        gv_ref[:, spot] = dot(scores, d, ((0,), (0,))).astype(BF16)

    half_room = pltpu.VMEM((rows, half_wide), BF16)

    def middle_own(ready, _):
        def kernel(
            stats_ref, mixed_own_ref, mixed_away_ref, d_ref, prefix_ref, q_any, k_any, v_any,
            out_any, gq_ref, gk_ref, gv_ref, q_ref, k_ref, v_ref, in_sems, out_own_ref, out_away_ref, out_sems,
        ):
            half = Half(OWN, heads)
            copies = loads(half, (q_any, k_any, v_any), (q_ref, k_ref, v_ref), in_sems)
            for part in copies:
                start(part)
            rstd, _ = token_scales(stats_ref)
            outs = []
            for which, mixed_ref, out_ref in ((OWN, mixed_own_ref, out_own_ref), (AWAY, mixed_away_ref, out_away_ref)):
                for spot in spots:
                    out_ref[:, spot] = (mixed_ref[:, spot] * rstd).astype(BF16)
                there = out_any.at[:, Half(which, heads).columns()]
                outs.append(pltpu.make_async_copy(out_ref, there, out_sems.at[which]))
                outs[-1].start()
            mask = causal(rows)
            for head, spot in enumerate(spots):
                if head % cut_heads == 0:
                    wait(copies[head // cut_heads])
                middle_head(
                    q_ref[:, spot], k_ref[:, spot], v_ref[:, spot], d_ref[:, spot], prefix_ref[spot, :], mask, spot,
                    gq_ref, gk_ref, gv_ref,
                )
            wait(outs)

        args = after(ready, stats, *mixed, d_own, prefix_own, query, key_in, value)
        scratch = [half_room] * 3 + [pltpu.SemaphoreType.DMA((cuts, 3))] + [half_room] * 2 + [pltpu.SemaphoreType.DMA((2,))]
        return call(kernel, [whole, packed, packed, packed], args, 5 * block_flops, (5, 6, 7), (0,), scratch, {3: 1})

    def middle_away(ready, _):
        def kernel(d_ref, prefix_ref, q_any, k_any, v_any, gq_ref, gk_ref, gv_ref, q_ref, k_ref, v_ref, in_sems):
            copies = loads(Half(AWAY, heads), (q_any, k_any, v_any), (q_ref, k_ref, v_ref), in_sems)
            for part in copies:
                start(part)
            mask = causal(rows)
            for head, spot in enumerate(spots):
                if head % cut_heads == 0:
                    wait(copies[head // cut_heads])
                middle_head(
                    q_ref[:, spot], k_ref[:, spot], v_ref[:, spot], d_ref[:, spot], prefix_ref[spot, :], mask, spot,
                    gq_ref, gk_ref, gv_ref,
                )

        args = after(ready, d_away, prefix_away, query, key_in, value)
        scratch = [half_room] * 3 + [pltpu.SemaphoreType.DMA((cuts, 3))]
        return call(kernel, [packed] * 3, args, 5 * block_flops, (2, 3, 4), (), scratch, {0: 0})

    def turn(ready, extra):
        def kernel(own_ref, away_ref, k_any, v_any, out_any, k_own_ref, v_own_ref, k_away_ref, v_away_ref, sems):
            copies = []
            for which, ref, k_ref, v_ref in ((OWN, own_ref, k_own_ref, v_own_ref), (AWAY, away_ref, k_away_ref, v_away_ref)):
                cols = Half(which, heads).columns()
                copies.append(pltpu.make_async_copy(k_any.at[:, cols], k_ref, sems.at[which, 0]))
                copies.append(pltpu.make_async_copy(v_any.at[:, cols], v_ref, sems.at[which, 1]))
                copies.append(pltpu.make_async_copy(ref, out_any.at[:, cols], sems.at[which, 2]))
            start(copies)
            wait(copies)

        args = after(ready, extra["gather"][1], extra["far"][0], key_in, value)
        scratch = [pltpu.SemaphoreType.DMA((2, 3))]
        return call(kernel, [whole] + [packed] * 4, args, width * rows, (2, 3), (0,), scratch)

    beside = {"gather": middle_own, "far": middle_away, "back": turn}
    g_own, g_away, extra = scan(g_keep, g_send, True, beside)
    output, _, *near_own = extra["gather"]
    _, *near_away = extra["far"]
    grad_q, *known = extra["back"]

    gives = 2
    give_heads, give_wide = half_heads // gives, half_wide // gives

    def last(which, suffix, so_far):
        def kernel(k_ref, v_ref, near_k_ref, near_v_ref, suffix_ref, *refs):
            gk_any, gv_any, gk_ref, gv_ref, sems = refs[len(so_far) :]
            half = Half(which, heads)
            copies = []
            for head, spot in enumerate(spots):
                state = half.get(suffix_ref, head)
                gk_ref[:, spot] = (near_k_ref[:, spot] + dot(v_ref[:, spot], state, ((1,), (1,)))).astype(BF16)
                gv_ref[:, spot] = (near_v_ref[:, spot] + dot(k_ref[:, spot], state, ((1,), (0,)))).astype(BF16)
                if (head + 1) % give_heads == 0:
                    cut = head // give_heads
                    here = pl.ds(cut * give_wide, give_wide)
                    there = half.columns(cut * give_wide, give_wide)
                    for j, (ref, out) in enumerate(((gk_ref, gk_any), (gv_ref, gv_any))):
                        copies.append(pltpu.make_async_copy(ref.at[:, here], out.at[:, there], sems.at[cut, j]))
                        copies[-1].start()
            wait(copies)

        args = (*known[2 * which : 2 * which + 2], *(near_own, near_away)[which], suffix, *so_far)
        return call(
            kernel,
            [whole, whole],
            args,
            2 * state_flops,
            tuple(5 + i for i in range(len(so_far))),
            (0, 1),
            [pltpu.VMEM((rows, half_wide), BF16)] * 2 + [pltpu.SemaphoreType.DMA((gives, 2))],
            {5 + i: i for i in range(len(so_far))},
        )

    grad_k, grad_v = last(AWAY, g_away, tuple(last(OWN, g_own, ())))
    return output, grad_q, grad_k, grad_v


def solution(mesh):
    spec = P("seq", "head")
    return jax.shard_map(local, mesh=mesh, in_specs=(spec,) * 4, out_specs=(spec,) * 4, check_vma=False)
```

```python
import jax
import jax.numpy as jnp
from jax import lax
from jax.experimental import pallas as pl
from jax.experimental.pallas import tpu as pltpu
from jax.sharding import PartitionSpec as P

HEAD_DIM = 128
EPS = 1e-06
F32 = jnp.float32
BF16 = jnp.bfloat16
VMEM = pl.BlockSpec(memory_space=pltpu.VMEM)
HBM = pl.BlockSpec(memory_space=pltpu.HBM)
OWN, AWAY = 0, 1

PIECES = 4
ORDER = {"gather": (1, 2, 3), "back": (2, 1, 3)}


def crosses(bits):
    return (bits & 1) ^ (bits >> 1)


def split(block):
    return block & 1, (block >> 1) & (PIECES - 1), block >> 3


class Half:
    def __init__(self, which, heads):
        core, self.team, _ = split(lax.axis_index("seq"))
        own = core ^ crosses(self.team)
        number = own if which == OWN else 1 - own
        self.heads = heads // 2
        self.base = number * (self.heads * HEAD_DIM)
        self.piece_rows = self.heads * HEAD_DIM // PIECES

    def columns(self, start=0, size=None):
        size = self.heads * HEAD_DIM if size is None else size
        return pl.ds(pl.multiple_of(self.base + start, HEAD_DIM), size)

    def state_parts(self, head):
        step = min(self.piece_rows, HEAD_DIM)
        return [
            ((head * HEAD_DIM + row) // self.piece_rows ^ self.team, (head * HEAD_DIM + row) % self.piece_rows, row, step)
            for row in range(0, HEAD_DIM, step)
        ]

    def put(self, ref, head, state):
        for place, there, here, step in self.state_parts(head):
            ref[place, there : there + step, :] = state[here : here + step, :]

    def get(self, ref, head):
        parts = [ref[place, there : there + step, :] for place, there, _, step in self.state_parts(head)]
        return (parts[0] if len(parts) == 1 else jnp.concatenate(parts, axis=0)).astype(BF16)


def dot(a, b, contract):
    return lax.dot_general(a, b, (contract, ((), ())), preferred_element_type=F32)


def causal(rows):
    return lax.broadcasted_iota(jnp.int32, (rows, rows), 0) >= lax.broadcasted_iota(jnp.int32, (rows, rows), 1)


def like(shape, dtype=F32):
    return jax.ShapeDtypeStruct(tuple(shape), dtype)


def call(kernel, outs, args, flops, in_hbm=(), out_hbm=(), scratch=(), alias=None):
    moved = sum(a.size * a.dtype.itemsize for a in (*args, *outs))
    return pl.pallas_call(
        kernel,
        out_shape=outs,
        in_specs=[HBM if i in in_hbm else VMEM for i in range(len(args))],
        out_specs=[HBM if i in out_hbm else VMEM for i in range(len(outs))],
        scratch_shapes=list(scratch),
        input_output_aliases=alias or {},
        cost_estimate=pl.CostEstimate(flops=int(flops), bytes_accessed=int(moved), transcendentals=0),
        compiler_params=pltpu.CompilerParams(vmem_limit_bytes=16 * 1024 * 1024),
    )(*[pltpu.with_memory_space_constraint(a, pltpu.HBM) if i in in_hbm else a for i, a in enumerate(args)])


def exchange(axis, partner, array):
    return lax.ppermute(array, axis, [(i, partner(i)) for i in range(lax.axis_size(axis))])


def after(early, *arrays):
    return lax.optimization_barrier((early, arrays))[1]


def scan(keep, send, reverse, beside):
    count = lax.axis_size("seq")
    core, team, far = split(lax.axis_index("seq"))
    if reverse:
        core, team, far = 1 - core, PIECES - 1 - team, count // 8 - 1 - far
    extra = {}

    def beside_of(name, ready, come):
        if name in beside:
            come, extra[name] = lax.optimization_barrier((come, beside[name](ready, extra)))
        return come

    def to_team(pieces, name):
        come = {0: pieces[0]}
        for r in ORDER[name]:
            come[r] = exchange("seq", lambda i: i ^ (2 * r) ^ crosses(r), pieces[r])
        come[r] = beside_of(name, pieces[r], come[r])
        return [come[r] for r in range(PIECES)]

    got = exchange("seq", lambda i: i ^ 1, send)
    both = keep + got
    edge = lax.optimization_barrier(jnp.where(core == 0, keep, got))
    parts = to_team([both[r] for r in range(PIECES)], "gather")
    total = parts[0] + parts[1] + (parts[2] + parts[3])

    before = jnp.zeros_like(total)
    steps = count // 8
    hop = 1
    while hop < steps:
        if steps & (steps - 1) == 0:
            come = exchange("seq", lambda i: i ^ (8 * hop), total)
            earlier = jnp.where(far & hop != 0, come, 0.0)
        else:
            up = [(i, i + 8 * hop) for i in range(count - 8 * hop)]
            come = lax.ppermute(total, "seq", [(d, s) for s, d in up] if reverse else up)
            earlier = come
        if 2 * hop >= steps:
            come, earlier = beside_of("far", total, (come, earlier))
        before = before + earlier
        total = total + come
        hop *= 2

    starts = []
    for r in range(PIECES):
        start = before
        for other in range(PIECES):
            if other != r:
                start = start + jnp.where((team ^ other) < (team ^ r), parts[other], 0.0)
        starts.append(start)
    base = jnp.stack(to_team(starts, "back"))
    away = exchange("seq", lambda i: i ^ 1, base + jnp.where(core == 0, edge, 0.0))
    own = base + jnp.where(core == 1, edge, 0.0)
    return own, away, extra


def local(query, key_in, value, cotangent):
    rows, width = query.shape
    heads = width // HEAD_DIM
    features = width * lax.axis_size("head")
    half_heads, half_wide = heads // 2, width // 2
    state_flops = heads * rows * HEAD_DIM * HEAD_DIM
    block_flops = heads * rows * rows * HEAD_DIM
    whole = like((rows, width), BF16)
    packed = like((rows, half_wide), BF16)
    wide = like((rows, half_wide))
    states = like((PIECES, half_heads * HEAD_DIM // PIECES, HEAD_DIM))
    spots = [pl.ds(head * HEAD_DIM, HEAD_DIM) for head in range(half_heads)]
    cuts = 1
    cut_heads = half_heads // cuts
    cut_wide = half_wide // cuts

    def loads(half, sources, targets, sems):
        return [
            [
                pltpu.make_async_copy(a.at[:, half.columns(cut * cut_wide, cut_wide)], b.at[:, pl.ds(cut * cut_wide, cut_wide)], sems.at[cut, j])
                for j, (a, b) in enumerate(zip(sources, targets))
            ]
            for cut in range(cuts)
        ]

    def start(copies):
        for copy in copies:
            copy.start()

    def wait(copies):
        for copy in copies:
            copy.wait()

    def first_states(k_any, v_any, k_own_ref, v_own_ref, k_ref, v_ref, out_ref, own_sems, sems):
        half = Half(AWAY, heads)
        near = loads(Half(OWN, heads), (k_any, v_any), (k_own_ref, v_own_ref), own_sems)
        copies = loads(half, (k_any, v_any), (k_ref, v_ref), sems)
        for part in copies + near:
            start(part)
        for head, spot in enumerate(spots):
            if head % cut_heads == 0:
                wait(copies[head // cut_heads])
            half.put(out_ref, head, dot(k_ref[:, spot], v_ref[:, spot], ((0,), (0,))))
        for part in near:
            wait(part)

    k_own, v_own, k_away, v_away, send = call(
        first_states,
        [packed] * 4 + [states],
        (key_in, value),
        state_flops,
        (0, 1),
        (),
        [pltpu.SemaphoreType.DMA((cuts, 2))] * 2,
    )

    def second_states(k_ref, v_ref, out_ref):
        half = Half(OWN, heads)
        for head, spot in enumerate(spots):
            half.put(out_ref, head, dot(k_ref[:, spot], v_ref[:, spot], ((0,), (0,))))

    (keep,) = call(second_states, [states], (k_own, v_own), state_flops)

    def inner(ready, _):
        def kernel(q_ref, *refs):
            mask = causal(rows)
            for which in (OWN, AWAY):
                half = Half(which, heads)
                k_ref, v_ref, near_ref = refs[which], refs[2 + which], refs[4 + which]
                for head, spot in enumerate(spots):
                    q = q_ref[:, half.columns(head * HEAD_DIM, HEAD_DIM)]
                    scores = jnp.where(mask, dot(q, k_ref[:, spot], ((1,), (1,))), 0.0).astype(BF16)
                    near_ref[:, spot] = dot(scores, v_ref[:, spot], ((1,), (0,)))

        args = after(ready, query, k_own, k_away, v_own, v_away)
        return call(kernel, [wide] * 2, args, 4 * block_flops)

    def bring(ready, _):
        def kernel(c_any, own_ref, away_ref, sems):
            copies = [
                pltpu.make_async_copy(c_any.at[:, Half(which, heads).columns()], ref, sems.at[which])
                for which, ref in ((OWN, own_ref), (AWAY, away_ref))
            ]
            start(copies)
            wait(copies)

        return call(kernel, [packed] * 2, after(ready, cotangent), width * rows, (0,), (), [pltpu.SemaphoreType.DMA((2,))])

    own, away, extra = scan(keep, send, False, {"far": inner, "back": bring})
    near, cots = extra["far"], extra["back"]

    def mix(which, prefix, so_far):
        def kernel(q_ref, c_ref, near_ref, prefix_ref, *refs):
            so_far_refs, (mixed_ref, stats_ref, rounded_ref) = refs[:-3], refs[-3:]
            half = Half(which, heads)
            square = jnp.zeros((rows, HEAD_DIM), F32)
            along = jnp.zeros((rows, HEAD_DIM), F32)
            for head, spot in enumerate(spots):
                cols = half.columns(head * HEAD_DIM, HEAD_DIM)
                prefix_b = half.get(prefix_ref, head)
                rounded_ref[spot, :] = prefix_b
                mixed = near_ref[:, spot] + dot(q_ref[:, cols], prefix_b, ((1,), (0,)))
                mixed_ref[:, spot] = mixed
                square += mixed * mixed
                along += c_ref[:, spot].astype(F32) * mixed
            stats_ref[0:1, :] = jnp.sum(square.T, axis=0, keepdims=True)
            stats_ref[1:2, :] = jnp.sum(along.T, axis=0, keepdims=True)
            for ref in so_far_refs:
                stats_ref[...] += ref[...]

        args = (query, cots[which], near[which], prefix, *([] if so_far is None else [so_far]))
        outs = [wide, like((2, rows)), like((half_wide, HEAD_DIM), BF16)]
        return call(kernel, outs, args, state_flops, alias={2: 0})

    mixed_own, stats_own, prefix_own = mix(OWN, own, None)
    mixed_away, stats, prefix_away = mix(AWAY, away, stats_own)
    mixed = (mixed_own, mixed_away)
    if lax.axis_size("head") == 2:
        sums = (stats, exchange("head", lambda i: 1 - i, stats))
    else:
        sums = (lax.psum(stats, "head"),)

    def token_scales(stats_refs):
        stats = sum(ref[...] for ref in stats_refs)
        rstd = lax.rsqrt(stats[0:1, :] / features + EPS)
        slope = rstd * rstd * (stats[1:2, :] / features)
        return (
            jnp.broadcast_to(rstd, (HEAD_DIM, rows)).T,
            jnp.broadcast_to(slope, (HEAD_DIM, rows)).T,
        )

    def grads(which):
        def kernel(q_ref, c_ref, mixed_ref, *refs):
            stats_refs, (d_ref, out_ref) = refs[:-2], refs[-2:]
            half = Half(which, heads)
            rstd, slope = token_scales(stats_refs)
            for head, spot in enumerate(spots):
                cols = half.columns(head * HEAD_DIM, HEAD_DIM)
                d_mixed = (rstd * (c_ref[:, spot].astype(F32) - mixed_ref[:, spot] * slope)).astype(BF16)
                d_ref[:, spot] = d_mixed
                half.put(out_ref, head, dot(q_ref[:, cols], d_mixed, ((0,), (0,))))

        return call(kernel, [packed, states], (query, cots[which], mixed[which], *sums), state_flops, alias={1: 0})

    d_away, g_send = grads(AWAY)
    d_own, g_keep = grads(OWN)

    def middle_head(q, k, v, d, prefix, mask, spot, gq_ref, gk_ref, gv_ref):
        scores = jnp.where(mask, dot(q, k, ((1,), (1,))), 0.0).astype(BF16)
        d_scores = jnp.where(mask, dot(d, v, ((1,), (1,))), 0.0).astype(BF16)
        gq_ref[:, spot] = (dot(d_scores, k, ((1,), (0,))) + dot(d, prefix, ((1,), (1,)))).astype(BF16)
        gk_ref[:, spot] = dot(d_scores, q, ((0,), (0,))).astype(BF16)
        gv_ref[:, spot] = dot(scores, d, ((0,), (0,))).astype(BF16)

    half_room = pltpu.VMEM((rows, half_wide), BF16)

    def middle_own(ready, _):
        def kernel(mixed_own_ref, mixed_away_ref, d_ref, prefix_ref, q_any, k_any, v_any, *refs):
            stats_refs, refs = refs[: len(sums)], refs[len(sums) :]
            out_any, gq_ref, gk_ref, gv_ref, q_ref, k_ref, v_ref, in_sems, out_own_ref, out_away_ref, out_sems = refs
            half = Half(OWN, heads)
            copies = loads(half, (q_any, k_any, v_any), (q_ref, k_ref, v_ref), in_sems)
            for part in copies:
                start(part)
            rstd, _ = token_scales(stats_refs)
            outs = []
            for which, mixed_ref, out_ref in ((OWN, mixed_own_ref, out_own_ref), (AWAY, mixed_away_ref, out_away_ref)):
                for spot in spots:
                    out_ref[:, spot] = (mixed_ref[:, spot] * rstd).astype(BF16)
                there = out_any.at[:, Half(which, heads).columns()]
                outs.append(pltpu.make_async_copy(out_ref, there, out_sems.at[which]))
                outs[-1].start()
            mask = causal(rows)
            for head, spot in enumerate(spots):
                if head % cut_heads == 0:
                    wait(copies[head // cut_heads])
                middle_head(
                    q_ref[:, spot], k_ref[:, spot], v_ref[:, spot], d_ref[:, spot], prefix_ref[spot, :], mask, spot,
                    gq_ref, gk_ref, gv_ref,
                )
            wait(outs)

        args = after(ready, *mixed, d_own, prefix_own, query, key_in, value, *sums)
        scratch = [half_room] * 3 + [pltpu.SemaphoreType.DMA((cuts, 3))] + [half_room] * 2 + [pltpu.SemaphoreType.DMA((2,))]
        return call(kernel, [whole, packed, packed, packed], args, 5 * block_flops, (4, 5, 6), (0,), scratch, {2: 1})

    def middle_away(ready, _):
        def kernel(d_ref, prefix_ref, q_any, k_any, v_any, gq_ref, gk_ref, gv_ref, q_ref, k_ref, v_ref, in_sems):
            copies = loads(Half(AWAY, heads), (q_any, k_any, v_any), (q_ref, k_ref, v_ref), in_sems)
            for part in copies:
                start(part)
            mask = causal(rows)
            for head, spot in enumerate(spots):
                if head % cut_heads == 0:
                    wait(copies[head // cut_heads])
                middle_head(
                    q_ref[:, spot], k_ref[:, spot], v_ref[:, spot], d_ref[:, spot], prefix_ref[spot, :], mask, spot,
                    gq_ref, gk_ref, gv_ref,
                )

        args = after(ready, d_away, prefix_away, query, key_in, value)
        scratch = [half_room] * 3 + [pltpu.SemaphoreType.DMA((cuts, 3))]
        return call(kernel, [packed] * 3, args, 5 * block_flops, (2, 3, 4), (), scratch, {0: 0})

    def turn(ready, extra):
        def kernel(own_ref, away_ref, k_any, v_any, out_any, k_own_ref, v_own_ref, k_away_ref, v_away_ref, sems):
            copies = []
            for which, ref, k_ref, v_ref in ((OWN, own_ref, k_own_ref, v_own_ref), (AWAY, away_ref, k_away_ref, v_away_ref)):
                cols = Half(which, heads).columns()
                copies.append(pltpu.make_async_copy(k_any.at[:, cols], k_ref, sems.at[which, 0]))
                copies.append(pltpu.make_async_copy(v_any.at[:, cols], v_ref, sems.at[which, 1]))
                copies.append(pltpu.make_async_copy(ref, out_any.at[:, cols], sems.at[which, 2]))
            start(copies)
            wait(copies)

        args = after(ready, extra["gather"][1], extra["far"][0], key_in, value)
        scratch = [pltpu.SemaphoreType.DMA((2, 3))]
        return call(kernel, [whole] + [packed] * 4, args, width * rows, (2, 3), (0,), scratch)

    beside = {"gather": middle_own, "far": middle_away, "back": turn}
    g_own, g_away, extra = scan(g_keep, g_send, True, beside)
    output, _, *near_own = extra["gather"]
    _, *near_away = extra["far"]
    grad_q, *known = extra["back"]

    gives = 2
    give_heads, give_wide = half_heads // gives, half_wide // gives

    def last(which, suffix, so_far):
        def kernel(k_ref, v_ref, near_k_ref, near_v_ref, suffix_ref, *refs):
            gk_any, gv_any, gk_ref, gv_ref, sems = refs[len(so_far) :]
            half = Half(which, heads)
            copies = []
            for head, spot in enumerate(spots):
                state = half.get(suffix_ref, head)
                gk_ref[:, spot] = (near_k_ref[:, spot] + dot(v_ref[:, spot], state, ((1,), (1,)))).astype(BF16)
                gv_ref[:, spot] = (near_v_ref[:, spot] + dot(k_ref[:, spot], state, ((1,), (0,)))).astype(BF16)
                if (head + 1) % give_heads == 0:
                    cut = head // give_heads
                    here = pl.ds(cut * give_wide, give_wide)
                    there = half.columns(cut * give_wide, give_wide)
                    for j, (ref, out) in enumerate(((gk_ref, gk_any), (gv_ref, gv_any))):
                        copies.append(pltpu.make_async_copy(ref.at[:, here], out.at[:, there], sems.at[cut, j]))
                        copies[-1].start()
            wait(copies)

        args = (*known[2 * which : 2 * which + 2], *(near_own, near_away)[which], suffix, *so_far)
        return call(
            kernel,
            [whole, whole],
            args,
            2 * state_flops,
            tuple(5 + i for i in range(len(so_far))),
            (0, 1),
            [pltpu.VMEM((rows, half_wide), BF16)] * 2 + [pltpu.SemaphoreType.DMA((gives, 2))],
            {5 + i: i for i in range(len(so_far))},
        )

    grad_k, grad_v = last(AWAY, g_away, tuple(last(OWN, g_own, ())))
    return output, grad_q, grad_k, grad_v


def solution(mesh):
    spec = P("seq", "head")
    return jax.shard_map(local, mesh=mesh, in_specs=(spec,) * 4, out_specs=(spec,) * 4, check_vma=False)
```

```python
import jax
import jax.numpy as jnp
from jax import lax
from jax.experimental import pallas as pl
from jax.experimental.pallas import tpu as pltpu
from jax.sharding import PartitionSpec as P

HEAD_DIM = 128
EPS = 1e-06
F32 = jnp.float32
BF16 = jnp.bfloat16
VMEM = pl.BlockSpec(memory_space=pltpu.VMEM)
HBM = pl.BlockSpec(memory_space=pltpu.HBM)
OWN, AWAY = 0, 1

PIECES = 4
ORDER = {"gather": (1, 2, 3), "back": (2, 1, 3)}


def crosses(bits):
    return (bits & 1) ^ (bits >> 1)


def split(block):
    return block & 1, (block >> 1) & (PIECES - 1), block >> 3


class Half:
    def __init__(self, which, heads):
        core, self.team, _ = split(lax.axis_index("seq"))
        own = core ^ crosses(self.team)
        number = own if which == OWN else 1 - own
        self.heads = heads // 2
        self.base = number * (self.heads * HEAD_DIM)
        self.piece_rows = self.heads * HEAD_DIM // PIECES

    def columns(self, start=0, size=None):
        size = self.heads * HEAD_DIM if size is None else size
        return pl.ds(pl.multiple_of(self.base + start, HEAD_DIM), size)

    def state_parts(self, head):
        step = min(self.piece_rows, HEAD_DIM)
        return [
            ((head * HEAD_DIM + row) // self.piece_rows ^ self.team, (head * HEAD_DIM + row) % self.piece_rows, row, step)
            for row in range(0, HEAD_DIM, step)
        ]

    def put(self, ref, head, state):
        for place, there, here, step in self.state_parts(head):
            ref[place, there : there + step, :] = state[here : here + step, :]

    def get(self, ref, head):
        parts = [ref[place, there : there + step, :] for place, there, _, step in self.state_parts(head)]
        return (parts[0] if len(parts) == 1 else jnp.concatenate(parts, axis=0)).astype(BF16)


def dot(a, b, contract):
    return lax.dot_general(a, b, (contract, ((), ())), preferred_element_type=F32)


def causal(rows):
    return lax.broadcasted_iota(jnp.int32, (rows, rows), 0) >= lax.broadcasted_iota(jnp.int32, (rows, rows), 1)


def like(shape, dtype=F32):
    return jax.ShapeDtypeStruct(tuple(shape), dtype)


def call(kernel, outs, args, flops, in_hbm=(), out_hbm=(), scratch=(), alias=None):
    moved = sum(a.size * a.dtype.itemsize for a in (*args, *outs))
    return pl.pallas_call(
        kernel,
        out_shape=outs,
        in_specs=[HBM if i in in_hbm else VMEM for i in range(len(args))],
        out_specs=[HBM if i in out_hbm else VMEM for i in range(len(outs))],
        scratch_shapes=list(scratch),
        input_output_aliases=alias or {},
        cost_estimate=pl.CostEstimate(flops=int(flops), bytes_accessed=int(moved), transcendentals=0),
        compiler_params=pltpu.CompilerParams(vmem_limit_bytes=16 * 1024 * 1024),
    )(*[pltpu.with_memory_space_constraint(a, pltpu.HBM) if i in in_hbm else a for i, a in enumerate(args)])


def exchange(axis, partner, array):
    return lax.ppermute(array, axis, [(i, partner(i)) for i in range(lax.axis_size(axis))])


def after(early, *arrays):
    return lax.optimization_barrier((early, arrays))[1]


def scan(keep, send, reverse, beside):
    count = lax.axis_size("seq")
    core, team, far = split(lax.axis_index("seq"))
    if reverse:
        core, team, far = 1 - core, PIECES - 1 - team, count // 8 - 1 - far
    extra = {}

    def beside_of(name, ready, come):
        if name in beside:
            come, extra[name] = lax.optimization_barrier((come, beside[name](ready, extra)))
        return come

    def to_team(pieces, name):
        come = {0: pieces[0]}
        for r in ORDER[name]:
            come[r] = exchange("seq", lambda i: i ^ (2 * r) ^ crosses(r), pieces[r])
        come[r] = beside_of(name, pieces[r], come[r])
        return [come[r] for r in range(PIECES)]

    got = exchange("seq", lambda i: i ^ 1, send)
    both = keep + got
    edge = lax.optimization_barrier(jnp.where(core == 0, keep, got))
    parts = to_team([both[r] for r in range(PIECES)], "gather")
    total = parts[0] + parts[1] + (parts[2] + parts[3])

    before = jnp.zeros_like(total)
    steps = count // 8
    hop = 1
    while hop < steps:
        if steps & (steps - 1) == 0:
            come = exchange("seq", lambda i: i ^ (8 * hop), total)
            earlier = jnp.where(far & hop != 0, come, 0.0)
        else:
            up = [(i, i + 8 * hop) for i in range(count - 8 * hop)]
            come = lax.ppermute(total, "seq", [(d, s) for s, d in up] if reverse else up)
            earlier = come
        if 2 * hop >= steps:
            come, earlier = beside_of("far", total, (come, earlier))
        before = before + earlier
        total = total + come
        hop *= 2

    starts = []
    for r in range(PIECES):
        start = before
        for other in range(PIECES):
            if other != r:
                start = start + jnp.where((team ^ other) < (team ^ r), parts[other], 0.0)
        starts.append(start)
    base = jnp.stack(to_team(starts, "back"))
    away = exchange("seq", lambda i: i ^ 1, base + jnp.where(core == 0, edge, 0.0))
    own = base + jnp.where(core == 1, edge, 0.0)
    return own, away, extra


def local(query, key_in, value, cotangent):
    rows, width = query.shape
    heads = width // HEAD_DIM
    features = width * lax.axis_size("head")
    half_heads, half_wide = heads // 2, width // 2
    state_flops = heads * rows * HEAD_DIM * HEAD_DIM
    block_flops = heads * rows * rows * HEAD_DIM
    whole = like((rows, width), BF16)
    packed = like((rows, half_wide), BF16)
    wide = like((rows, half_wide))
    states = like((PIECES, half_heads * HEAD_DIM // PIECES, HEAD_DIM))
    spots = [pl.ds(head * HEAD_DIM, HEAD_DIM) for head in range(half_heads)]
    cuts = 1
    cut_heads = half_heads // cuts
    cut_wide = half_wide // cuts

    def loads(half, sources, targets, sems):
        return [
            [
                pltpu.make_async_copy(a.at[:, half.columns(cut * cut_wide, cut_wide)], b.at[:, pl.ds(cut * cut_wide, cut_wide)], sems.at[cut, j])
                for j, (a, b) in enumerate(zip(sources, targets))
            ]
            for cut in range(cuts)
        ]

    def start(copies):
        for copy in copies:
            copy.start()

    def wait(copies):
        for copy in copies:
            copy.wait()

    def first_states(k_any, v_any, k_own_ref, v_own_ref, k_ref, v_ref, out_ref, own_sems, sems):
        half = Half(AWAY, heads)
        near = loads(Half(OWN, heads), (k_any, v_any), (k_own_ref, v_own_ref), own_sems)
        copies = loads(half, (k_any, v_any), (k_ref, v_ref), sems)
        for part in copies + near:
            start(part)
        for head, spot in enumerate(spots):
            if head % cut_heads == 0:
                wait(copies[head // cut_heads])
            half.put(out_ref, head, dot(k_ref[:, spot], v_ref[:, spot], ((0,), (0,))))
        for part in near:
            wait(part)

    k_own, v_own, k_away, v_away, send = call(
        first_states,
        [packed] * 4 + [states],
        (key_in, value),
        state_flops,
        (0, 1),
        (),
        [pltpu.SemaphoreType.DMA((cuts, 2))] * 2,
    )

    def second_states(k_ref, v_ref, out_ref):
        half = Half(OWN, heads)
        for head, spot in enumerate(spots):
            half.put(out_ref, head, dot(k_ref[:, spot], v_ref[:, spot], ((0,), (0,))))

    (keep,) = call(second_states, [states], (k_own, v_own), state_flops)

    def inner(ready, _):
        def kernel(q_ref, *refs):
            mask = causal(rows)
            for which in (OWN, AWAY):
                half = Half(which, heads)
                k_ref, v_ref, near_ref = refs[which], refs[2 + which], refs[4 + which]
                for head, spot in enumerate(spots):
                    q = q_ref[:, half.columns(head * HEAD_DIM, HEAD_DIM)]
                    scores = jnp.where(mask, dot(q, k_ref[:, spot], ((1,), (1,))), 0.0).astype(BF16)
                    near_ref[:, spot] = dot(scores, v_ref[:, spot], ((1,), (0,)))

        args = after(ready, query, k_own, k_away, v_own, v_away)
        return call(kernel, [wide] * 2, args, 4 * block_flops)

    def bring(ready, _):
        def kernel(c_any, own_ref, away_ref, sems):
            copies = [
                pltpu.make_async_copy(c_any.at[:, Half(which, heads).columns()], ref, sems.at[which])
                for which, ref in ((OWN, own_ref), (AWAY, away_ref))
            ]
            start(copies)
            wait(copies)

        return call(kernel, [packed] * 2, after(ready, cotangent), width * rows, (0,), (), [pltpu.SemaphoreType.DMA((2,))])

    own, away, extra = scan(keep, send, False, {"far": inner, "back": bring})
    near, cots = extra["far"], extra["back"]

    def mix(which, prefix, so_far):
        def kernel(q_ref, c_ref, near_ref, prefix_ref, *refs):
            so_far_refs, (mixed_ref, stats_ref, rounded_ref) = refs[:-3], refs[-3:]
            half = Half(which, heads)
            square = jnp.zeros((rows, HEAD_DIM), F32)
            along = jnp.zeros((rows, HEAD_DIM), F32)
            for head, spot in enumerate(spots):
                cols = half.columns(head * HEAD_DIM, HEAD_DIM)
                prefix_b = half.get(prefix_ref, head)
                rounded_ref[spot, :] = prefix_b
                mixed = near_ref[:, spot] + dot(q_ref[:, cols], prefix_b, ((1,), (0,)))
                mixed_ref[:, spot] = mixed
                square += mixed * mixed
                along += c_ref[:, spot].astype(F32) * mixed
            fold = HEAD_DIM // 2
            left = lax.broadcasted_iota(jnp.int32, (rows, HEAD_DIM), 1) < fold
            both = jnp.where(left, square, along) + pltpu.roll(jnp.where(left, along, square), fold, 1)
            both = both.T
            stats_ref[0:1, :] = jnp.sum(both[:fold], axis=0, keepdims=True)
            stats_ref[1:2, :] = jnp.sum(both[fold:], axis=0, keepdims=True)
            for ref in so_far_refs:
                stats_ref[...] += ref[...]

        args = (query, cots[which], near[which], prefix, *([] if so_far is None else [so_far]))
        outs = [wide, like((2, rows)), like((half_wide, HEAD_DIM), BF16)]
        return call(kernel, outs, args, state_flops, alias={2: 0})

    mixed_own, stats_own, prefix_own = mix(OWN, own, None)
    mixed_away, stats, prefix_away = mix(AWAY, away, stats_own)
    mixed = (mixed_own, mixed_away)
    if lax.axis_size("head") == 2:
        sums = (stats, exchange("head", lambda i: 1 - i, stats))
    else:
        sums = (lax.psum(stats, "head"),)

    def token_scales(stats_refs):
        stats = sum(ref[...] for ref in stats_refs)
        rstd = lax.rsqrt(stats[0:1, :] / features + EPS)
        slope = rstd * rstd * (stats[1:2, :] / features)
        return (
            jnp.broadcast_to(rstd, (HEAD_DIM, rows)).T,
            jnp.broadcast_to(slope, (HEAD_DIM, rows)).T,
        )

    def grads(which):
        def kernel(q_ref, c_ref, mixed_ref, *refs):
            stats_refs, (d_ref, out_ref) = refs[:-2], refs[-2:]
            half = Half(which, heads)
            rstd, slope = token_scales(stats_refs)
            for head, spot in enumerate(spots):
                cols = half.columns(head * HEAD_DIM, HEAD_DIM)
                d_mixed = (rstd * (c_ref[:, spot].astype(F32) - mixed_ref[:, spot] * slope)).astype(BF16)
                d_ref[:, spot] = d_mixed
                half.put(out_ref, head, dot(q_ref[:, cols], d_mixed, ((0,), (0,))))

        return call(kernel, [packed, states], (query, cots[which], mixed[which], *sums), state_flops, alias={1: 0})

    d_away, g_send = grads(AWAY)
    d_own, g_keep = grads(OWN)

    def middle_head(q, k, v, d, prefix, mask, spot, gq_ref, gk_ref, gv_ref):
        scores = jnp.where(mask, dot(q, k, ((1,), (1,))), 0.0).astype(BF16)
        d_scores = jnp.where(mask, dot(d, v, ((1,), (1,))), 0.0).astype(BF16)
        gq_ref[:, spot] = (dot(d_scores, k, ((1,), (0,))) + dot(d, prefix, ((1,), (1,)))).astype(BF16)
        gk_ref[:, spot] = dot(d_scores, q, ((0,), (0,))).astype(BF16)
        gv_ref[:, spot] = dot(scores, d, ((0,), (0,))).astype(BF16)

    half_room = pltpu.VMEM((rows, half_wide), BF16)

    def middle_own(ready, _):
        def kernel(mixed_own_ref, mixed_away_ref, d_ref, prefix_ref, q_any, k_any, v_any, *refs):
            stats_refs, refs = refs[: len(sums)], refs[len(sums) :]
            out_any, gq_ref, gk_ref, gv_ref, q_ref, k_ref, v_ref, in_sems, out_own_ref, out_away_ref, out_sems = refs
            half = Half(OWN, heads)
            copies = loads(half, (q_any, k_any, v_any), (q_ref, k_ref, v_ref), in_sems)
            for part in copies:
                start(part)
            rstd, _ = token_scales(stats_refs)
            outs = []
            for which, mixed_ref, out_ref in ((OWN, mixed_own_ref, out_own_ref), (AWAY, mixed_away_ref, out_away_ref)):
                for spot in spots:
                    out_ref[:, spot] = (mixed_ref[:, spot] * rstd).astype(BF16)
                there = out_any.at[:, Half(which, heads).columns()]
                outs.append(pltpu.make_async_copy(out_ref, there, out_sems.at[which]))
                outs[-1].start()
            mask = causal(rows)
            for head, spot in enumerate(spots):
                if head % cut_heads == 0:
                    wait(copies[head // cut_heads])
                middle_head(
                    q_ref[:, spot], k_ref[:, spot], v_ref[:, spot], d_ref[:, spot], prefix_ref[spot, :], mask, spot,
                    gq_ref, gk_ref, gv_ref,
                )
            wait(outs)

        args = after(ready, *mixed, d_own, prefix_own, query, key_in, value, *sums)
        scratch = [half_room] * 3 + [pltpu.SemaphoreType.DMA((cuts, 3))] + [half_room] * 2 + [pltpu.SemaphoreType.DMA((2,))]
        return call(kernel, [whole, packed, packed, packed], args, 5 * block_flops, (4, 5, 6), (0,), scratch, {2: 1})

    def middle_away(ready, _):
        def kernel(d_ref, prefix_ref, q_any, k_any, v_any, gq_ref, gk_ref, gv_ref, q_ref, k_ref, v_ref, in_sems):
            copies = loads(Half(AWAY, heads), (q_any, k_any, v_any), (q_ref, k_ref, v_ref), in_sems)
            for part in copies:
                start(part)
            mask = causal(rows)
            for head, spot in enumerate(spots):
                if head % cut_heads == 0:
                    wait(copies[head // cut_heads])
                middle_head(
                    q_ref[:, spot], k_ref[:, spot], v_ref[:, spot], d_ref[:, spot], prefix_ref[spot, :], mask, spot,
                    gq_ref, gk_ref, gv_ref,
                )

        args = after(ready, d_away, prefix_away, query, key_in, value)
        scratch = [half_room] * 3 + [pltpu.SemaphoreType.DMA((cuts, 3))]
        return call(kernel, [packed] * 3, args, 5 * block_flops, (2, 3, 4), (), scratch, {0: 0})

    def turn(ready, extra):
        def kernel(own_ref, away_ref, k_any, v_any, out_any, k_own_ref, v_own_ref, k_away_ref, v_away_ref, sems):
            copies = []
            for which, ref, k_ref, v_ref in ((OWN, own_ref, k_own_ref, v_own_ref), (AWAY, away_ref, k_away_ref, v_away_ref)):
                cols = Half(which, heads).columns()
                copies.append(pltpu.make_async_copy(k_any.at[:, cols], k_ref, sems.at[which, 0]))
                copies.append(pltpu.make_async_copy(v_any.at[:, cols], v_ref, sems.at[which, 1]))
                copies.append(pltpu.make_async_copy(ref, out_any.at[:, cols], sems.at[which, 2]))
            start(copies)
            wait(copies)

        args = after(ready, extra["gather"][1], extra["far"][0], key_in, value)
        scratch = [pltpu.SemaphoreType.DMA((2, 3))]
        return call(kernel, [whole] + [packed] * 4, args, width * rows, (2, 3), (0,), scratch)

    beside = {"gather": middle_own, "far": middle_away, "back": turn}
    g_own, g_away, extra = scan(g_keep, g_send, True, beside)
    output, _, *near_own = extra["gather"]
    _, *near_away = extra["far"]
    grad_q, *known = extra["back"]

    gives = 2
    give_heads, give_wide = half_heads // gives, half_wide // gives

    def last(which, suffix, so_far):
        def kernel(k_ref, v_ref, near_k_ref, near_v_ref, suffix_ref, *refs):
            gk_any, gv_any, gk_ref, gv_ref, sems = refs[len(so_far) :]
            half = Half(which, heads)
            copies = []
            for head, spot in enumerate(spots):
                state = half.get(suffix_ref, head)
                gk_ref[:, spot] = (near_k_ref[:, spot] + dot(v_ref[:, spot], state, ((1,), (1,)))).astype(BF16)
                gv_ref[:, spot] = (near_v_ref[:, spot] + dot(k_ref[:, spot], state, ((1,), (0,)))).astype(BF16)
                if (head + 1) % give_heads == 0:
                    cut = head // give_heads
                    here = pl.ds(cut * give_wide, give_wide)
                    there = half.columns(cut * give_wide, give_wide)
                    for j, (ref, out) in enumerate(((gk_ref, gk_any), (gv_ref, gv_any))):
                        copies.append(pltpu.make_async_copy(ref.at[:, here], out.at[:, there], sems.at[cut, j]))
                        copies[-1].start()
            wait(copies)

        args = (*known[2 * which : 2 * which + 2], *(near_own, near_away)[which], suffix, *so_far)
        return call(
            kernel,
            [whole, whole],
            args,
            2 * state_flops,
            tuple(5 + i for i in range(len(so_far))),
            (0, 1),
            [pltpu.VMEM((rows, half_wide), BF16)] * 2 + [pltpu.SemaphoreType.DMA((gives, 2))],
            {5 + i: i for i in range(len(so_far))},
        )

    grad_k, grad_v = last(AWAY, g_away, tuple(last(OWN, g_own, ())))
    return output, grad_q, grad_k, grad_v


def solution(mesh):
    spec = P("seq", "head")
    return jax.shard_map(local, mesh=mesh, in_specs=(spec,) * 4, out_specs=(spec,) * 4, check_vma=False)
```
